32 devices in a mesh: src: 8 (over y, x, core), tgt: 4 (over z).
Axes of the slice: x: 2, y: 2, z: 4, core: 2. Of those that a mesh axis runs over, the one named last changes fastest.
Arguments:
- feature_a: bfloat16 [16, 128, 1024], P('src', 'tgt'), may hold values from -6 to 6
- feature_b: bfloat16 [8, 16, 1024], P('tgt', 'src'), may hold values from -6 to 6
- conv_in: float32 [8, 81], replicated, may hold values from -0.625 to 0.625
- bias_in: float32 [8], replicated, may hold values from -4 to 4
- conv_out: float32 [8, 81], replicated, may hold values from -0.25 to 0.25
Outputs:
- consensus: float32 [8, 16, 16, 128], P('tgt', 'src')
The draws below stay inside these ranges and needn't reach their ends.
All inputs are finite; a program needn't handle non-finite values.
Results may differ from the reference program's by a relative error of at most 0.0024.
Values may be sent and summed in bfloat16 or wider, within the bound.
A program may use at most 64 MiB of HBM per device.

```python
import jax
import jax.numpy as jnp
from jax import lax

C = 1024
CH = 8
WA = 128
HA = 16
HB = 8
WB = 16


def level_of(stream_key, dims, shards, low, high):
    def one(position, parts):
        steps = jax.random.uniform(jax.random.fold_in(jax.random.fold_in(stream_key, 6), position), (parts,), jnp.float32, low / len(shards), high / len(shards))
        return jnp.repeat(jnp.exp(steps), dims[position] // parts).reshape((-1,) + (1,) * (len(dims) - position - 1))

    loudness = one(*shards[0])
    for cut in shards[1:]:
        loudness = loudness * one(*cut)
    return loudness


def normal_values(stream_key, shape, scale, reach, split=(), kind=jnp.bfloat16):
    result = jax.random.normal(stream_key, shape, jnp.float32) * scale
    if len(split) > 0:
        result = level_of(stream_key, shape, split, -0.22, 0.18) * result
    return jnp.clip(result, min=-reach, max=reach).astype(kind)


def setup_inputs(seed: int = 0) -> dict:
    key_list = jax.random.split(jax.random.key(seed), 6)
    return {
        "feature_a": normal_values(key_list[0], (HA, WA, C), 1.0, 6.0, ((0, 8), (1, 4))),
        "feature_b": normal_values(key_list[1], (HB, WB, C), 1.0, 6.0, ((0, 4), (1, 8))),
        "conv_in": normal_values(key_list[2], (CH, 81), 81 ** -0.5, 0.625, (), jnp.float32),
        "bias_in": normal_values(key_list[3], (CH,), 1.0, 4.0, (), jnp.float32),
        "conv_out": normal_values(key_list[4], (CH, 81), (81 * CH) ** -0.5, 0.25, (), jnp.float32),
    }


def filter_taps(source, weights, extent):
    summed_total = jnp.zeros(extent, jnp.float32)
    for first in range(3):
        for second in range(3):
            for third in range(3):
                for fourth in range(3):
                    weight = weights[first * 27 + second * 9 + third * 3 + fourth]
                    summed_total = summed_total + weight * source[first:first + extent[0], second:second + extent[1], third:third + extent[2], fourth:fourth + extent[3]]
    return summed_total


def network(volume, conv_in, bias_in, conv_out):
    extent = volume.shape
    field = jnp.pad(volume, 1)

    def channel_step(channel_slot, summed_total):
        hidden = jax.nn.relu(filter_taps(field, conv_in[channel_slot], extent) + bias_in[channel_slot])
        padded = jnp.pad(hidden, 1)
        return summed_total + filter_taps(padded, conv_out[channel_slot], extent)

    return lax.fori_loop(0, conv_in.shape[0], channel_step, jnp.zeros(extent, jnp.float32))


def reference(feature_a, feature_b, conv_in, bias_in, conv_out):
    scores = jnp.dot(feature_b.reshape(HB * WB, C), feature_a.reshape(HA * WA, C).T, preferred_element_type=jnp.float32)
    volume = (scores * (C ** -0.5)).astype(jnp.bfloat16).astype(jnp.float32).reshape(HB, WB, HA, WA)
    forward = network(volume, conv_in, bias_in, conv_out)
    mirrored = network(volume.transpose(2, 3, 0, 1), conv_in, bias_in, conv_out).transpose(2, 3, 0, 1)
    return forward + mirrored
```

```python
import functools

import jax
import jax.numpy as jnp
import numpy as np
from jax import lax
from jax.experimental import pallas as pl
from jax.experimental.pallas import tpu as pltpu
from jax.sharding import PartitionSpec as P

LANES = 128
F32 = jnp.float32
BF16 = jnp.bfloat16


def round_up(value, unit):
    return -(-value // unit) * unit


class Plan:
    def __init__(self, count_s, count_t, a_shape, b_shape, hidden):
        self.S, self.T = count_s, count_t
        self.rows_i, self.cols_j, self.C = a_shape
        self.kb, self.lb = b_shape[0], b_shape[1]
        self.hidden = hidden
        self.ij = self.rows_i * self.cols_j
        self.HA = self.rows_i * count_s
        self.WA = self.cols_j * count_t
        assert self.WA == LANES and LANES % self.ij == 0 and LANES // self.ij >= self.kb
        self.nk, self.nl = -(-2 // self.kb), -(-2 // self.lb)
        self.bk, self.bl = 2 * self.nk + 1, 2 * self.nl + 1
        self.L = self.bl * self.lb
        self.half = round_up(self.bk * self.L + 1, 8)
        self.KX = round_up(self.kb * self.half, 16)
        self.KP = 9 * self.KX
        self.KW = round_up(self.KP, LANES)
        self.hk, self.hl = self.kb + 2, self.lb + 2
        self.M = self.hk * self.hl * 2 * hidden
        self.unit = round_up(self.kb * self.lb, 8)
        self.Y = round_up(9 * self.unit, 16)
        assert self.Y <= LANES

    def tap(self, net, p, q, r, s):
        p, q, r, s = (p, q, r, s) if net == 0 else (r, s, p, q)
        return 27 * p + 9 * q + 3 * r + s

    def select_in(self):
        out = np.zeros((LANES, self.kb, 2, self.KW), np.float32)
        for par in range(self.kb):
            for net in range(2):
                for p, q, r, s in np.ndindex(3, 3, 3, 3):
                    ek = par + p - 2 + self.nk * self.kb
                    el = q - 2 + self.nl * self.lb
                    col = (r * 3 + s) * self.KX + (ek % self.kb) * self.half
                    col += (ek // self.kb) * self.L + el
                    out[self.tap(net, p, q, r, s), par, net, col] = 1
        return out.reshape(LANES, -1)

    def select_out(self):
        out = np.zeros((LANES, self.hk, self.hl, 2, LANES), np.float32)
        for k, l, net in np.ndindex(self.hk, self.hl, 2):
            for ok, ol, r, s in np.ndindex(self.kb, self.lb, 3, 3):
                p, q = k - ok, l - ol
                if 0 <= p < 3 and 0 <= q < 3:
                    col = (r * 3 + s) * self.unit + ok * self.lb + ol
                    out[self.tap(net, p, q, r, s), k, l, net, col] = 1
        return out.reshape(LANES, -1)


def split(x):
    high = x.astype(BF16)
    return high, (x - high.astype(F32)).astype(BF16)


def dot(x, y):
    return jnp.dot(x, y, preferred_element_type=F32)


def iota(shape, dim):
    return lax.broadcasted_iota(jnp.int32, shape, dim)


def kernel(
    g, a_hbm, b_ref, cin_ref, bias_ref, cout_ref, s1_hbm, s2_hbm, out_ref,
    a_vm, s1_vm, s2_vm, load_sem, bb, bf, vs, vp, rb, u, pat, w1h, w1l, w2h, w2l, y, cpad,
    s_a1, s_a2, r_a, s_b, r_b,
):
    S, T = g.S, g.T
    N = S * T
    s = lax.axis_index("src")
    t = lax.axis_index("tgt")
    me = s * T + t

    loads = [
        pltpu.make_async_copy(a_hbm, a_vm, load_sem.at[0]),
        pltpu.make_async_copy(s1_hbm, s1_vm, load_sem.at[1]),
        pltpu.make_async_copy(s2_hbm, s2_vm, load_sem.at[2]),
    ]
    for load in loads:
        load.start()

    barrier = pltpu.get_barrier_semaphore()

    @pl.loop(1, N)
    def _(n):
        other = lax.rem(me + n, N)
        pl.semaphore_signal(
            barrier, inc=1, device_id={"src": other // T, "tgt": lax.rem(other, T)},
            device_id_type=pl.DeviceIdType.MESH,
        )

    bb[s, t] = b_ref[...]
    vp[...] = jnp.zeros(vp.shape, BF16)
    pl.semaphore_wait(barrier, N - 1)

    def piece(ps, pt, send, ds, dt):
        return pltpu.make_async_remote_copy(
            src_ref=bb.at[ps, pt], dst_ref=bb.at[ps, pt], send_sem=send,
            recv_sem=r_a.at[ps, pt], device_id={"src": ds, "tgt": dt},
            device_id_type=pl.DeviceIdType.MESH,
        )

    def to_row(m, n):
        return piece(s, lax.rem(t + m, T), s_a2.at[m, n], lax.rem(s + n, S), t)

    def to_column(m):
        return piece(s, t, s_a1.at[m], s, lax.rem(t + m, T))

    @pl.loop(1, T)
    def _(m):
        to_column(m).start()

    @pl.loop(1, S)
    def _(n):
        to_row(0, n).start()

    @pl.loop(1, T)
    def _(m):
        piece(s, lax.rem(t + m, T), s_a1.at[m], s, lax.rem(t + m, T)).wait_recv()

        @pl.loop(1, S)
        def _(n):
            to_row(m, n).start()

    loads[1].wait()
    cpad[...] = jnp.zeros(cpad.shape, F32)
    cpad[:, : cin_ref.shape[1]] = cin_ref[...]
    taps_h, taps_l = split(cpad[...])
    both = jnp.concatenate([taps_h.astype(F32), taps_l.astype(F32)], axis=0).astype(BF16)
    base = dot(both, s1_vm[...])
    H = g.hidden
    row = iota((H, LANES), 0)
    bias = jnp.zeros((H, LANES), F32)
    for h in range(H):
        bias = jnp.where(row == h, bias_ref[h], bias)
    bias_h, bias_l = (part.astype(F32) for part in split(bias))
    bias = jnp.concatenate([bias_h, bias_h, bias_l, bias_l], axis=0)
    bias = jnp.concatenate([bias] * (g.KW // LANES), axis=1)
    bias = jnp.where(iota(bias.shape, 1) == 4 * g.KX + g.half - 1, bias, 0.0)
    for k in range(g.hk):
        at_k = t * g.kb + (k - 1)
        for l in range(g.hl):
            at_l = s * g.lb + (l - 1)
            parts = []
            for first in (0, H):
                for net in range(2):
                    at = ((k % g.kb) * 2 + net) * g.KW
                    parts.append(base[first : first + H, at : at + g.KW])
            block = jnp.concatenate(parts, axis=0)
            shift = (k // g.kb) * g.L + l
            if shift:
                block = pltpu.roll(block, shift, 1)
            inside = (at_k >= 0) & (at_k < T * g.kb) & (at_l >= 0) & (at_l < S * g.lb)
            block = (block + bias) * jnp.where(inside, 1.0, 0.0).astype(F32)
            at = (k * g.hl + l) * 2 * H
            w1h[at : at + 2 * H, :] = block[: 2 * H, : g.KP].astype(BF16)
            w1l[at : at + 2 * H, :] = block[2 * H :, : g.KP].astype(BF16)

    loads[2].wait()
    cpad[:, : cout_ref.shape[1]] = cout_ref[...]
    taps_h, taps_l = split(cpad[...])
    both = jnp.concatenate([taps_h.astype(F32), taps_l.astype(F32)], axis=0).astype(BF16)
    base = dot(both, s2_vm[...])
    blocks = g.hk * g.hl * 2
    for first, ref in ((0, w2h), (H, w2l)):
        tall = jnp.concatenate(
            [base[first : first + H, n * LANES : (n + 1) * LANES] for n in range(blocks)], axis=0
        )
        ref[...] = tall.T[: g.Y].astype(BF16)

    tail = g.half - g.bk * g.L
    u[:, g.bk * g.L :, :] = jnp.where(
        iota((T, tail, LANES), 1) == tail - 1, jnp.ones((T, tail, LANES), F32), 0.0
    )
    pat[: 3 * g.KX, LANES : 2 * LANES] = jnp.zeros((3 * g.KX, LANES), BF16)
    pat[6 * g.KX :, g.HA * LANES : (g.HA + 1) * LANES] = jnp.zeros((3 * g.KX, LANES), BF16)
    y[:, :LANES] = jnp.zeros((g.Y, LANES), F32)
    y[:, (g.HA + 1) * LANES :] = jnp.zeros((g.Y, LANES), F32)

    loads[0].wait()
    a = a_vm[...].astype(F32).reshape(g.ij, g.C)
    a = jnp.concatenate([a] * (LANES // g.ij), axis=0).astype(BF16)

    def take(ps):
        for tt in range(T):
            for kk in range(g.kb):
                bf[kk, ps, tt * g.lb : (tt + 1) * g.lb, :] = bb[ps, tt, kk].astype(F32)

    take(s)

    @pl.loop(1, S)
    def _(n):
        ps = lax.rem(s + n, S)

        @pl.loop(0, T)
        def _(m):
            pt = lax.rem(t + m, T)
            piece(ps, pt, s_a2.at[m, n], ps, t).wait_recv()

        take(ps)

    total = S * T * g.lb
    targets = bf[...].reshape(g.kb * total, g.C).astype(BF16)
    scores = lax.dot_general(
        targets, a, (((1,), (1,)), ((), ())), preferred_element_type=F32
    ) * (g.C ** -0.5)
    volume = scores[:total]
    for kk in range(1, g.kb):
        volume = jnp.where(
            iota((total, LANES), 1) >= kk * g.ij, scores[kk * total : (kk + 1) * total], volume
        )
    vs[...] = volume.reshape(S, T * g.lb, LANES)

    @pl.loop(0, S)
    def _(ps):
        for tt in range(T):
            vp[ps + g.nl, tt + g.nk] = vs[ps, tt * g.lb : (tt + 1) * g.lb, :].astype(BF16)

    def block_to(n):
        other = lax.rem(me + n, N)
        os, ot = other // T, lax.rem(other, T)
        return pltpu.make_async_remote_copy(
            src_ref=vp.at[pl.ds(os, g.bl), pl.ds(ot, g.bk)], dst_ref=rb.at[s, t],
            send_sem=s_b.at[n], recv_sem=r_b.at[s, t],
            device_id={"src": os, "tgt": ot}, device_id_type=pl.DeviceIdType.MESH,
        )

    @pl.loop(1, N)
    def _(n):
        block_to(n).start()

    rb[s, t] = vp[pl.ds(s, g.bl), pl.ds(t, g.bk)]

    lane = iota((g.half, LANES), 1)
    wide = iota((g.kb * g.half, LANES), 1)

    def spread(ps):
        for tt in range(T):
            for dt in range(g.bk):
                for ds in range(g.bl):
                    at = dt * g.L + ds * g.lb
                    u[tt, at : at + g.lb, :] = rb[ps, tt, ds, dt].astype(F32)
        ins = [u[tt] for tt in range(T)]
        for ii in range(g.rows_i):
            parts = []
            for kk in range(g.kb):
                chunk = kk * g.rows_i + ii
                joined = None
                for tt in range(T):
                    shift = (tt - chunk) * g.cols_j % LANES
                    moved = pltpu.roll(ins[tt], shift, 1) if shift else ins[tt]
                    joined = moved if tt == 0 else jnp.where(lane >= tt * g.cols_j, moved, joined)
                parts.append(joined)
            x = jnp.concatenate(parts, axis=0)
            if g.KX > x.shape[0]:
                x = jnp.concatenate([x, jnp.zeros((g.KX - x.shape[0], LANES), F32)], axis=0)
            for sh in range(3):
                if sh == 0:
                    moved = jnp.where(iota(x.shape, 1) == 0, 0.0, pltpu.roll(x, 1, 1))
                elif sh == 2:
                    moved = jnp.where(
                        iota(x.shape, 1) == LANES - 1, 0.0, pltpu.roll(x, LANES - 1, 1)
                    )
                else:
                    moved = x
                moved = moved.astype(BF16)
                for r in range(3):
                    at = pl.multiple_of((ps * g.rows_i + (ii + 2 - r)) * LANES, LANES)
                    first = (r * 3 + sh) * g.KX
                    pat[first : first + g.KX, pl.ds(at, LANES)] = moved

    def arrive(ps, pt):
        pltpu.make_async_remote_copy(
            src_ref=rb.at[ps, pt], dst_ref=rb.at[ps, pt], send_sem=s_b.at[0],
            recv_sem=r_b.at[ps, pt], device_id={"src": ps, "tgt": pt},
            device_id_type=pl.DeviceIdType.MESH,
        ).wait_recv()

    @pl.loop(1, T)
    def _(m):
        arrive(s, lax.rem(t + m, T))

    spread(s)

    @pl.loop(1, S)
    def _(n):
        ps = lax.rem(s + n, S)

        @pl.loop(0, T)
        def _(m):
            arrive(ps, lax.rem(t + m, T))

        spread(ps)

    chunk = 4 * LANES

    @pl.loop(0, g.HA * LANES // chunk)
    def _(n):
        at = pl.multiple_of(LANES + n * chunk, LANES)
        patch = pat[:, pl.ds(at, chunk)]
        hid = jnp.maximum(dot(w1h[...], patch) + dot(w1l[...], patch), 0.0)
        hid_h, hid_l = split(hid)
        y[:, pl.ds(at, chunk)] = (
            dot(w2h[...], hid_h) + dot(w2l[...], hid_h) + dot(w2h[...], hid_l)
        )

    last = iota((g.unit, LANES), 1)
    for i in range(g.HA):
        sums = []
        for sh in range(3):
            part = None
            for r in range(3):
                first = (r * 3 + sh) * g.unit
                term = y[first : first + g.unit, (i + r) * LANES : (i + r + 1) * LANES]
                part = term if part is None else part + term
            sums.append(part)
        res = sums[1]
        res = res + jnp.where(last == 0, 0.0, pltpu.roll(sums[0], 1, 1))
        res = res + jnp.where(last == LANES - 1, 0.0, pltpu.roll(sums[2], LANES - 1, 1))
        for k in range(g.kb):
            for l in range(g.lb):
                n = k * g.lb + l
                out_ref[k, l, i : i + 1, :] = res[n : n + 1, :]

    @pl.loop(1, T)
    def _(m):
        to_column(m).wait_send()

    @pl.loop(0, T)
    def _(m):
        @pl.loop(1, S)
        def _(n):
            to_row(m, n).wait_send()

    @pl.loop(1, N)
    def _(n):
        block_to(n).wait_send()


def per_device(feature_a, feature_b, conv_in, bias_in, conv_out):
    S, T = lax.axis_size("src"), lax.axis_size("tgt")
    g = Plan(S, T, feature_a.shape, feature_b.shape, conv_in.shape[0])
    s1 = jnp.asarray(g.select_in(), BF16)
    s2 = jnp.asarray(g.select_out(), BF16)
    vm = pl.BlockSpec(memory_space=pltpu.VMEM)
    hbm = pl.BlockSpec(memory_space=pl.ANY)
    dma = pltpu.SemaphoreType.DMA
    return pl.pallas_call(
        functools.partial(kernel, g),
        out_shape=jax.ShapeDtypeStruct((g.kb, g.lb, g.HA, g.WA), F32),
        in_specs=[hbm, vm, vm, pl.BlockSpec(memory_space=pltpu.SMEM), vm, hbm, hbm],
        out_specs=vm,
        scratch_shapes=[
            pltpu.VMEM(feature_a.shape, BF16),
            pltpu.VMEM(s1.shape, BF16),
            pltpu.VMEM(s2.shape, BF16),
            dma((3,)),
            pltpu.VMEM((S, T, g.kb, g.lb, g.C), BF16),
            pltpu.VMEM((g.kb, S, T * g.lb, g.C), F32),
            pltpu.VMEM((S, T * g.lb, LANES), F32),
            pltpu.VMEM((S + 2 * g.nl, T + 2 * g.nk, g.lb, LANES), BF16),
            pltpu.VMEM((S, T, g.bl, g.bk, g.lb, LANES), BF16),
            pltpu.VMEM((T, g.half, LANES), F32),
            pltpu.VMEM((g.KP, (g.HA + 2) * LANES), BF16),
            pltpu.VMEM((g.M, g.KP), BF16),
            pltpu.VMEM((g.M, g.KP), BF16),
            pltpu.VMEM((g.Y, g.M), BF16),
            pltpu.VMEM((g.Y, g.M), BF16),
            pltpu.VMEM((g.Y, (g.HA + 2) * LANES), F32),
            pltpu.VMEM((g.hidden, LANES), F32),
            dma((T,)),
            dma((T, S)),
            dma((S, T)),
            dma((S * T,)),
            dma((S, T)),
        ],
        compiler_params=pltpu.CompilerParams(
            collective_id=0, has_side_effects=True, vmem_limit_bytes=44 * 1024 * 1024
        ),
    )(feature_a, feature_b, conv_in, bias_in, conv_out, s1, s2)


def solution(mesh):
    in_specs = (P("src", "tgt", None), P("tgt", "src", None), P(), P(), P())
    out_specs = P("tgt", "src", None, None)
    return jax.shard_map(
        per_device, mesh=mesh, in_specs=in_specs, out_specs=out_specs, check_vma=False
    )
```

```python
import functools

import jax
import jax.numpy as jnp
import numpy as np
from jax import lax
from jax.experimental import pallas as pl
from jax.experimental.pallas import tpu as pltpu
from jax.sharding import PartitionSpec as P

LANES = 128
F32 = jnp.float32
BF16 = jnp.bfloat16


def round_up(value, unit):
    return -(-value // unit) * unit


class Plan:
    def __init__(self, count_s, count_t, a_shape, b_shape, hidden):
        self.S, self.T = count_s, count_t
        self.rows_i, self.cols_j, self.C = a_shape
        self.kb, self.lb = b_shape[0], b_shape[1]
        self.hidden = hidden
        self.ij = self.rows_i * self.cols_j
        self.HA = self.rows_i * count_s
        self.WA = self.cols_j * count_t
        assert self.WA == LANES and LANES % self.ij == 0 and LANES // self.ij >= self.kb
        self.nk, self.nl = -(-2 // self.kb), -(-2 // self.lb)
        self.bk, self.bl = 2 * self.nk + 1, 2 * self.nl + 1
        self.L = self.bl * self.lb
        self.half = round_up(self.bk * self.L + 1, 8)
        self.KX = round_up(self.kb * self.half, 16)
        self.KP = 9 * self.KX
        self.KW = round_up(self.KP, LANES)
        self.hk, self.hl = self.kb + 2, self.lb + 2
        self.M = self.hk * self.hl * 2 * hidden
        self.unit = round_up(self.kb * self.lb, 8)
        self.Y = round_up(9 * self.unit, 16)
        assert self.Y <= LANES

    def tap(self, net, p, q, r, s):
        p, q, r, s = (p, q, r, s) if net == 0 else (r, s, p, q)
        return 27 * p + 9 * q + 3 * r + s

    def select_in(self):
        out = np.zeros((LANES, self.kb, 2, self.KW), np.float32)
        for par in range(self.kb):
            for net in range(2):
                for p, q, r, s in np.ndindex(3, 3, 3, 3):
                    ek = par + p - 2 + self.nk * self.kb
                    el = q - 2 + self.nl * self.lb
                    col = (r * 3 + s) * self.KX + (ek % self.kb) * self.half
                    col += (ek // self.kb) * self.L + el
                    out[self.tap(net, p, q, r, s), par, net, col] = 1
        return out.reshape(LANES, -1)

    def select_out(self):
        out = np.zeros((LANES, self.hk, self.hl, 2, LANES), np.float32)
        for k, l, net in np.ndindex(self.hk, self.hl, 2):
            for ok, ol, r, s in np.ndindex(self.kb, self.lb, 3, 3):
                p, q = k - ok, l - ol
                if 0 <= p < 3 and 0 <= q < 3:
                    col = (r * 3 + s) * self.unit + ok * self.lb + ol
                    out[self.tap(net, p, q, r, s), k, l, net, col] = 1
        return out.reshape(LANES, -1)


def split(x):
    high = x.astype(BF16)
    return high, (x - high.astype(F32)).astype(BF16)


def dot(x, y):
    return jnp.dot(x, y, preferred_element_type=F32)


def iota(shape, dim):
    return lax.broadcasted_iota(jnp.int32, shape, dim)


def kernel(
    g, a_hbm, b_hbm, cin_hbm, bias_hbm, cout_hbm, s1_hbm, s2_hbm, out_ref,
    a_vm, b_ref, cin_ref, bias_ref, cout_ref, s1_vm, s2_vm, load_sem,
    bb, bf, vs, vp, rb, u, pat, w1h, w1l, w2h, w2l, y, cpad,
    s_a1, s_a2, r_a1, r_a2, s_b1, s_b2, r_b,
):
    S, T = g.S, g.T
    N = S * T
    s = lax.axis_index("src")
    t = lax.axis_index("tgt")
    me = s * T + t

    loads = [
        pltpu.make_async_copy(src, dst, load_sem.at[n])
        for n, (src, dst) in enumerate((
            (b_hbm, b_ref), (cin_hbm, cin_ref), (bias_hbm, bias_ref), (s1_hbm, s1_vm),
            (cout_hbm, cout_ref), (s2_hbm, s2_vm), (a_hbm, a_vm),
        ))
    ]
    for load in loads:
        load.start()

    barrier = pltpu.get_barrier_semaphore()

    def greet(ps, pt):
        pl.semaphore_signal(
            barrier, inc=1, device_id={"src": ps, "tgt": pt}, device_id_type=pl.DeviceIdType.MESH
        )

    for m in range(1, T):
        greet(s, lax.rem(t + m, T))
    for n in range(1, S):
        greet(lax.rem(s + n, S), t)
    loads[0].wait()
    bb[s, t] = b_ref[...]
    vp[...] = jnp.zeros(vp.shape, BF16)
    pl.semaphore_wait(barrier, S + T - 2)

    def piece(pt, send, recv, ds, dt):
        return pltpu.make_async_remote_copy(
            src_ref=bb.at[s, pt], dst_ref=bb.at[s, pt], send_sem=send, recv_sem=recv,
            device_id={"src": ds, "tgt": dt}, device_id_type=pl.DeviceIdType.MESH,
        )

    def taken(ref, sem):
        pltpu.make_async_copy(ref, ref, sem).wait()

    def to_row(pt):
        for n in range(1, S):
            piece(pt, s_a2.at[0], r_a2.at[s], lax.rem(s + n, S), t).start()

    for m in range(1, T):
        piece(t, s_a1.at[0], r_a1.at[t], s, lax.rem(t + m, T)).start()
    to_row(t)
    for m in range(1, T):
        pt = lax.rem(t + m, T)
        taken(bb.at[s, pt], r_a1.at[pt])
        to_row(pt)

    for load in loads[1:4]:
        load.wait()
    cpad[...] = jnp.zeros(cpad.shape, F32)
    cpad[:, : cin_ref.shape[1]] = cin_ref[...]
    taps_h, taps_l = split(cpad[...])
    both = jnp.concatenate([taps_h.astype(F32), taps_l.astype(F32)], axis=0).astype(BF16)
    base = dot(both, s1_vm[...])
    H = g.hidden
    row = iota((H, LANES), 0)
    bias = jnp.zeros((H, LANES), F32)
    for h in range(H):
        bias = jnp.where(row == h, bias_ref[h], bias)
    bias_h, bias_l = (part.astype(F32) for part in split(bias))
    bias = jnp.concatenate([bias_h, bias_h, bias_l, bias_l], axis=0)
    bias = jnp.concatenate([bias] * (g.KW // LANES), axis=1)
    bias = jnp.where(iota(bias.shape, 1) == 4 * g.KX + g.half - 1, bias, 0.0)
    for k in range(g.hk):
        at_k = t * g.kb + (k - 1)
        for l in range(g.hl):
            at_l = s * g.lb + (l - 1)
            parts = []
            for first in (0, H):
                for net in range(2):
                    at = ((k % g.kb) * 2 + net) * g.KW
                    parts.append(base[first : first + H, at : at + g.KW])
            block = jnp.concatenate(parts, axis=0)
            shift = (k // g.kb) * g.L + l
            if shift:
                block = pltpu.roll(block, shift, 1)
            inside = (at_k >= 0) & (at_k < T * g.kb) & (at_l >= 0) & (at_l < S * g.lb)
            block = (block + bias) * jnp.where(inside, 1.0, 0.0).astype(F32)
            at = (k * g.hl + l) * 2 * H
            w1h[at : at + 2 * H, :] = block[: 2 * H, : g.KP].astype(BF16)
            w1l[at : at + 2 * H, :] = block[2 * H :, : g.KP].astype(BF16)

    loads[4].wait()
    loads[5].wait()
    cpad[:, : cout_ref.shape[1]] = cout_ref[...]
    taps_h, taps_l = split(cpad[...])
    both = jnp.concatenate([taps_h.astype(F32), taps_l.astype(F32)], axis=0).astype(BF16)
    base = dot(both, s2_vm[...])
    blocks = g.hk * g.hl * 2
    for first, ref in ((0, w2h), (H, w2l)):
        tall = jnp.concatenate(
            [base[first : first + H, n * LANES : (n + 1) * LANES] for n in range(blocks)], axis=0
        )
        ref[...] = tall.T[: g.Y].astype(BF16)

    tail = g.half - g.bk * g.L
    u[:, g.bk * g.L :, :] = jnp.where(
        iota((T, tail, LANES), 1) == tail - 1, jnp.ones((T, tail, LANES), F32), 0.0
    )
    pat[: 3 * g.KX, LANES : 2 * LANES] = jnp.zeros((3 * g.KX, LANES), BF16)
    pat[6 * g.KX :, g.HA * LANES : (g.HA + 1) * LANES] = jnp.zeros((3 * g.KX, LANES), BF16)
    y[:, :LANES] = jnp.zeros((g.Y, LANES), F32)
    y[:, (g.HA + 1) * LANES :] = jnp.zeros((g.Y, LANES), F32)

    loads[6].wait()
    a = a_vm[...].astype(F32).reshape(g.ij, g.C)
    a = jnp.concatenate([a] * (LANES // g.ij), axis=0).astype(BF16)

    def take(ps):
        for tt in range(T):
            for kk in range(g.kb):
                bf[kk, ps, tt * g.lb : (tt + 1) * g.lb, :] = bb[ps, tt, kk].astype(F32)

    take(s)

    for n in range(1, S):
        ps = lax.rem(s + n, S)
        taken(bb.at[ps], r_a2.at[ps])
        take(ps)

    total = S * T * g.lb
    targets = bf[...].reshape(g.kb * total, g.C).astype(BF16)
    scores = lax.dot_general(
        targets, a, (((1,), (1,)), ((), ())), preferred_element_type=F32
    ) * (g.C ** -0.5)
    volume = scores[:total]
    for kk in range(1, g.kb):
        volume = jnp.where(
            iota((total, LANES), 1) >= kk * g.ij, scores[kk * total : (kk + 1) * total], volume
        )
    vs[...] = volume.reshape(S, T * g.lb, LANES)

    for ps in range(S):
        for tt in range(T):
            vp[ps + g.nl, tt + g.nk] = vs[ps, tt * g.lb : (tt + 1) * g.lb, :].astype(BF16)

    def block_to(ps, pt, send):
        pltpu.make_async_remote_copy(
            src_ref=vp.at[pl.ds(ps, g.bl), pl.ds(pt, g.bk)], dst_ref=rb.at[s, t],
            send_sem=send, recv_sem=r_b.at[s],
            device_id={"src": ps, "tgt": pt}, device_id_type=pl.DeviceIdType.MESH,
        ).start()

    for m in range(T - 1, -1, -1):
        pt = lax.rem(t + m, T)
        for n in range(S):
            if n:
                block_to(lax.rem(s + n, S), pt, s_b2.at[0])
            elif m:
                block_to(s, pt, s_b1.at[0])
    pltpu.make_async_copy(
        vp.at[pl.ds(s, g.bl), pl.ds(t, g.bk)], rb.at[s, t], r_b.at[s]
    ).start()
    taken(bb.at[0, : T - 1], s_a1.at[0])
    taken(bb.at[: S - 1], s_a2.at[0])

    lane = iota((g.half, LANES), 1)
    wide = iota((g.kb * g.half, LANES), 1)

    def spread(ps):
        for tt in range(T):
            for dt in range(g.bk):
                for ds in range(g.bl):
                    at = dt * g.L + ds * g.lb
                    u[tt, at : at + g.lb, :] = rb[ps, tt, ds, dt].astype(F32)
        ins = [u[tt] for tt in range(T)]
        for ii in range(g.rows_i):
            parts = []
            for kk in range(g.kb):
                chunk = kk * g.rows_i + ii
                joined = None
                for tt in range(T):
                    shift = (tt - chunk) * g.cols_j % LANES
                    moved = pltpu.roll(ins[tt], shift, 1) if shift else ins[tt]
                    joined = moved if tt == 0 else jnp.where(lane >= tt * g.cols_j, moved, joined)
                parts.append(joined)
            x = jnp.concatenate(parts, axis=0)
            if g.KX > x.shape[0]:
                x = jnp.concatenate([x, jnp.zeros((g.KX - x.shape[0], LANES), F32)], axis=0)
            for sh in range(3):
                if sh == 0:
                    moved = jnp.where(iota(x.shape, 1) == 0, 0.0, pltpu.roll(x, 1, 1))
                elif sh == 2:
                    moved = jnp.where(
                        iota(x.shape, 1) == LANES - 1, 0.0, pltpu.roll(x, LANES - 1, 1)
                    )
                else:
                    moved = x
                moved = moved.astype(BF16)
                for r in range(3):
                    at = (ps * g.rows_i + (ii + 2 - r)) * LANES
                    first = (r * 3 + sh) * g.KX
                    pat[first : first + g.KX, at : at + LANES] = moved

    def filters(ps):
        at, chunk = (1 + ps * g.rows_i) * LANES, g.rows_i * LANES
        patch = pat[:, at : at + chunk]
        hid = jnp.maximum(dot(w1h[...], patch) + dot(w1l[...], patch), 0.0)
        hid_h, hid_l = split(hid)
        y[:, at : at + chunk] = (
            dot(w2h[...], hid_h) + dot(w2l[...], hid_h) + dot(w2h[...], hid_l)
        )

    for ps in range(S):
        taken(rb.at[ps], r_b.at[ps])
        if ps == 1:
            taken(rb.at[0, : T - 1], s_b1.at[0])
            taken(rb.at[: S - 1], s_b2.at[0])
        spread(ps)
        if ps >= 2:
            filters(ps - 2)
    for ps in range(max(S - 2, 0), S):
        filters(ps)

    last = iota((g.unit, LANES), 1)
    for i in range(g.HA):
        sums = []
        for sh in range(3):
            part = None
            for r in range(3):
                first = (r * 3 + sh) * g.unit
                term = y[first : first + g.unit, (i + r) * LANES : (i + r + 1) * LANES]
                part = term if part is None else part + term
            sums.append(part)
        res = sums[1]
        res = res + jnp.where(last == 0, 0.0, pltpu.roll(sums[0], 1, 1))
        res = res + jnp.where(last == LANES - 1, 0.0, pltpu.roll(sums[2], LANES - 1, 1))
        for k in range(g.kb):
            for l in range(g.lb):
                n = k * g.lb + l
                out_ref[k, l, i : i + 1, :] = res[n : n + 1, :]


def per_device(feature_a, feature_b, conv_in, bias_in, conv_out):
    S, T = lax.axis_size("src"), lax.axis_size("tgt")
    g = Plan(S, T, feature_a.shape, feature_b.shape, conv_in.shape[0])
    s1 = jnp.asarray(g.select_in(), BF16)
    s2 = jnp.asarray(g.select_out(), BF16)
    vm = pl.BlockSpec(memory_space=pltpu.VMEM)
    hbm = pl.BlockSpec(memory_space=pl.ANY)
    dma = pltpu.SemaphoreType.DMA
    return pl.pallas_call(
        functools.partial(kernel, g),
        out_shape=jax.ShapeDtypeStruct((g.kb, g.lb, g.HA, g.WA), F32),
        in_specs=[hbm] * 7,
        out_specs=vm,
        scratch_shapes=[
            pltpu.VMEM(feature_a.shape, BF16),
            pltpu.VMEM(feature_b.shape, BF16),
            pltpu.VMEM(conv_in.shape, F32),
            pltpu.SMEM(bias_in.shape, F32),
            pltpu.VMEM(conv_out.shape, F32),
            pltpu.VMEM(s1.shape, BF16),
            pltpu.VMEM(s2.shape, BF16),
            dma((7,)),
            pltpu.VMEM((S, T, g.kb, g.lb, g.C), BF16),
            pltpu.VMEM((g.kb, S, T * g.lb, g.C), F32),
            pltpu.VMEM((S, T * g.lb, LANES), F32),
            pltpu.VMEM((S + 2 * g.nl, T + 2 * g.nk, g.lb, LANES), BF16),
            pltpu.VMEM((S, T, g.bl, g.bk, g.lb, LANES), BF16),
            pltpu.VMEM((T, g.half, LANES), F32),
            pltpu.VMEM((g.KP, (g.HA + 2) * LANES), BF16),
            pltpu.VMEM((g.M, g.KP), BF16),
            pltpu.VMEM((g.M, g.KP), BF16),
            pltpu.VMEM((g.Y, g.M), BF16),
            pltpu.VMEM((g.Y, g.M), BF16),
            pltpu.VMEM((g.Y, (g.HA + 2) * LANES), F32),
            pltpu.VMEM((g.hidden, LANES), F32),
            dma((1,)),
            dma((1,)),
            dma((T,)),
            dma((S,)),
            dma((1,)),
            dma((1,)),
            dma((S,)),
        ],
        compiler_params=pltpu.CompilerParams(
            collective_id=0, has_side_effects=True, vmem_limit_bytes=62 * 1024 * 1024
        ),
    )(feature_a, feature_b, conv_in, bias_in, conv_out, s1, s2)


def solution(mesh):
    in_specs = (P("src", "tgt", None), P("tgt", "src", None), P(), P(), P())
    out_specs = P("tgt", "src", None, None)
    return jax.shard_map(
        per_device, mesh=mesh, in_specs=in_specs, out_specs=out_specs, check_vma=False
    )
```

```python
import functools

import jax
import jax.numpy as jnp
import numpy as np
from jax import lax
from jax.experimental import pallas as pl
from jax.experimental.pallas import tpu as pltpu
from jax.sharding import PartitionSpec as P

LANES = 128
F32 = jnp.float32
BF16 = jnp.bfloat16


def round_up(value, unit):
    return -(-value // unit) * unit


class Plan:
    def __init__(self, count_s, count_t, a_shape, b_shape, hidden):
        self.S, self.T = count_s, count_t
        self.rows_i, self.cols_j, self.C = a_shape
        self.kb, self.lb = b_shape[0], b_shape[1]
        self.hidden = hidden
        self.G = 2
        assert count_s % self.G == 0
        self.H2 = count_s // self.G
        self.ij = self.rows_i * self.cols_j
        self.HA = self.rows_i * count_s
        self.WA = self.cols_j * count_t
        self.pair = self.G * self.ij
        assert self.WA == LANES and LANES % self.pair == 0 and self.kb >= 2 and self.lb >= 2
        self.bk = self.bl = 3
        self.block = self.kb * self.lb
        self.used = self.bk * self.bl * self.block
        self.rows = round_up(self.used + 1, 8)
        self.KX = round_up(self.rows, 16)
        self.KP = 9 * self.KX
        self.KW = round_up(self.KP, LANES)
        self.hk, self.hl = self.kb + 2, self.lb + 2
        self.M = self.hk * self.hl * 2 * hidden
        self.unit = round_up(self.block, 8)
        self.Y = round_up(9 * self.unit, 16)
        assert self.Y <= LANES

    def tap(self, net, p, q, r, s):
        p, q, r, s = (p, q, r, s) if net == 0 else (r, s, p, q)
        return 27 * p + 9 * q + 3 * r + s

    def select_in(self):
        out = np.zeros((LANES, self.kb, self.lb, 2, self.KW), np.float32)
        for k, l, net in np.ndindex(self.kb, self.lb, 2):
            for p, q, r, s in np.ndindex(3, 3, 3, 3):
                ek, el = k + p - 2 + self.kb, l + q - 2 + self.lb
                col = (r * 3 + s) * self.KX + (el % self.lb) + (ek % self.kb) * self.lb
                col += (el // self.lb * self.bk + ek // self.kb) * self.block
                out[self.tap(net, p, q, r, s), k, l, net, col] = 1
        return out.reshape(LANES, -1)

    def select_out(self):
        out = np.zeros((LANES, self.hk, self.hl, 2, LANES), np.float32)
        for k, l, net in np.ndindex(self.hk, self.hl, 2):
            for ok, ol, r, s in np.ndindex(self.kb, self.lb, 3, 3):
                p, q = k - ok, l - ol
                if 0 <= p < 3 and 0 <= q < 3:
                    col = (r * 3 + s) * self.unit + ok * self.lb + ol
                    out[self.tap(net, p, q, r, s), k, l, net, col] = 1
        return out.reshape(LANES, -1)


def split(x):
    high = x.astype(BF16)
    return high, (x - high.astype(F32)).astype(BF16)


def dot(x, y):
    return jnp.dot(x, y, preferred_element_type=F32)


def iota(shape, dim):
    return lax.broadcasted_iota(jnp.int32, shape, dim)


def kernel(
    g, a_hbm, b_hbm, cin_hbm, bias_hbm, cout_hbm, s1_hbm, s2_hbm, out_ref,
    ach, b_ref, cin_ref, bias_ref, cout_ref, s1_vm, s2_vm, load_sem,
    bb, bf, vs, vp, r1, r2, u, pat, w1h, w1l, w2h, w2l, y, cpad,
    s_x, r_x, s_a, r_a, s_b1, s_b2, r_b1, r_b2,
):
    S, T = g.S, g.T
    H2 = g.H2
    N = H2 * T
    s = lax.axis_index("src")
    t = lax.axis_index("tgt")
    core = lax.rem(s, g.G)
    h = s // g.G
    sibling = s + 1 - 2 * core

    loads = [
        pltpu.make_async_copy(src, dst, load_sem.at[n])
        for n, (src, dst) in enumerate((
            (b_hbm, b_ref), (cin_hbm, cin_ref), (bias_hbm, bias_ref), (s1_hbm, s1_vm),
            (cout_hbm, cout_ref), (s2_hbm, s2_vm), (a_hbm, ach.at[core]),
        ))
    ]
    for load in loads:
        load.start()

    barrier = pltpu.get_barrier_semaphore()

    def greet(ps, pt):
        pl.semaphore_signal(
            barrier, inc=1, device_id={"src": ps, "tgt": pt}, device_id_type=pl.DeviceIdType.MESH
        )

    peers = [
        (lax.rem(h + n, H2), lax.rem(t + m, T)) for n in range(H2) for m in range(T) if n or m
    ]
    greet(sibling, t)
    for ph, pt in peers:
        greet(ph * g.G + core, pt)
    loads[0].wait()
    vp[...] = jnp.zeros(vp.shape, BF16)
    pl.semaphore_wait(barrier, N)

    def remote(src, dst, send, recv, ps, pt):
        return pltpu.make_async_remote_copy(
            src_ref=src, dst_ref=dst, send_sem=send, recv_sem=recv,
            device_id={"src": ps, "tgt": pt}, device_id_type=pl.DeviceIdType.MESH,
        )

    def taken(ref, sem):
        pltpu.make_async_copy(ref, ref, sem).wait()

    for ph, pt in peers:
        remote(b_ref, bb.at[h, t], s_a.at[0], r_a.at[h], ph * g.G + core, pt).start()
    swap = remote(a_hbm, ach.at[core], s_x.at[0], r_x.at[0], sibling, t)
    swap.start()
    pltpu.make_async_copy(b_ref, bb.at[h, t], r_a.at[h]).start()

    for load in loads[1:4]:
        load.wait()
    cpad[...] = jnp.zeros(cpad.shape, F32)
    cpad[:, : cin_ref.shape[1]] = cin_ref[...]
    taps_h, taps_l = split(cpad[...])
    both = jnp.concatenate([taps_h.astype(F32), taps_l.astype(F32)], axis=0).astype(BF16)
    base = dot(both, s1_vm[...])
    H = g.hidden
    row = iota((H, LANES), 0)
    bias = jnp.zeros((H, LANES), F32)
    for n in range(H):
        bias = jnp.where(row == n, bias_ref[n], bias)
    bias_h, bias_l = (part.astype(F32) for part in split(bias))
    bias = jnp.concatenate([bias_h, bias_h, bias_l, bias_l], axis=0)
    bias = jnp.concatenate([bias] * (g.KW // LANES), axis=1)
    bias = jnp.where(iota(bias.shape, 1) == 4 * g.KX + g.rows - 1, bias, 0.0)
    for k in range(g.hk):
        at_k = t * g.kb + (k - 1)
        for l in range(g.hl):
            at_l = s * g.lb + (l - 1)
            parts = []
            for first in (0, H):
                for net in range(2):
                    at = ((k % g.kb * g.lb + l % g.lb) * 2 + net) * g.KW
                    parts.append(base[first : first + H, at : at + g.KW])
            block = jnp.concatenate(parts, axis=0)
            shift = (l // g.lb * g.bk + k // g.kb) * g.block
            if shift:
                block = pltpu.roll(block, shift, 1)
            inside = (at_k >= 0) & (at_k < T * g.kb) & (at_l >= 0) & (at_l < S * g.lb)
            block = (block + bias) * jnp.where(inside, 1.0, 0.0).astype(F32)
            at = (k * g.hl + l) * 2 * H
            w1h[at : at + 2 * H, :] = block[: 2 * H, : g.KP].astype(BF16)
            w1l[at : at + 2 * H, :] = block[2 * H :, : g.KP].astype(BF16)

    loads[4].wait()
    loads[5].wait()
    cpad[:, : cout_ref.shape[1]] = cout_ref[...]
    taps_h, taps_l = split(cpad[...])
    both = jnp.concatenate([taps_h.astype(F32), taps_l.astype(F32)], axis=0).astype(BF16)
    base = dot(both, s2_vm[...])
    blocks = g.hk * g.hl * 2
    for first, ref in ((0, w2h), (H, w2l)):
        tall = jnp.concatenate(
            [base[first : first + H, n * LANES : (n + 1) * LANES] for n in range(blocks)], axis=0
        )
        ref[...] = tall.T[: g.Y].astype(BF16)

    tail = g.rows - g.used
    u[:, :, g.used :, :] = jnp.where(
        iota((H2, T, tail, LANES), 2) == tail - 1, jnp.ones((H2, T, tail, LANES), F32), 0.0
    )
    pat[: 3 * g.KX, LANES : 2 * LANES] = jnp.zeros((3 * g.KX, LANES), BF16)
    pat[6 * g.KX :, g.HA * LANES : (g.HA + 1) * LANES] = jnp.zeros((3 * g.KX, LANES), BF16)
    y[:, :LANES] = jnp.zeros((g.Y, LANES), F32)
    y[:, (g.HA + 1) * LANES :] = jnp.zeros((g.Y, LANES), F32)

    loads[6].wait()
    swap.wait_recv()
    a = ach[...].astype(F32).reshape(g.pair, g.C)
    a = jnp.concatenate([a] * (LANES // g.pair), axis=0).astype(BF16)

    for n in range(H2):
        ph = lax.rem(h + n, H2)
        taken(bb.at[ph], r_a.at[ph])
        for tt in range(T):
            for kk in range(g.kb):
                at = tt * g.block + kk * g.lb
                bf[ph, at : at + g.lb, :] = bb[ph, tt, kk].astype(F32)

    total = N * g.block
    targets = bf[...].reshape(total, g.C).astype(BF16)
    volume = lax.dot_general(
        targets, a, (((1,), (1,)), ((), ())), preferred_element_type=F32
    ) * (g.C ** -0.5)
    vs[...] = volume.reshape(H2, T * g.block, LANES)
    for ph in range(H2):
        for tt in range(T):
            vp[ph + 1, tt + 1] = vs[ph, tt * g.block : (tt + 1) * g.block, :].astype(BF16)

    def near(ph, pt):
        return vp.at[pl.ds(ph + 1, 1), pl.ds(pt, g.bk)]

    def other(ph, pt):
        return vp.at[pl.ds(ph + 1 - core, 2), pl.ds(pt, g.bk)]

    for ph, pt in peers + [(h, t)]:
        remote(
            other(ph, pt), r2.at[h, t], s_b2.at[0], r_b2.at[h], ph * g.G + 1 - core, pt
        ).start()
    for ph, pt in peers:
        remote(near(ph, pt), r1.at[h, t], s_b1.at[0], r_b1.at[h], ph * g.G + core, pt).start()
    pltpu.make_async_copy(near(h, t), r1.at[h, t], r_b1.at[h]).start()
    for ph, pt in peers:
        pltpu.make_async_copy(b_ref, b_ref, s_a.at[0]).wait()
    swap.wait_send()

    lane = iota((g.rows, LANES), 1)
    wide = iota((g.KX, LANES), 1)
    rows_h = g.G * g.rows_i

    def spread(ph):
        ins = []
        for tt in range(T):
            for dt in range(g.bk):
                for ds in range(g.bl):
                    at = (ds * g.bk + dt) * g.block
                    got = r1[ph, tt, 0, dt] if ds == 1 else r2[ph, tt, ds // 2, dt]
                    u[ph, tt, at : at + g.block, :] = got.astype(F32)
            ins.append(u[ph, tt])
        for chunk in range(rows_h):
            x = None
            for tt in range(T):
                shift = (tt - chunk) * g.cols_j % LANES
                moved = pltpu.roll(ins[tt], shift, 1) if shift else ins[tt]
                x = moved if tt == 0 else jnp.where(lane >= tt * g.cols_j, moved, x)
            if g.KX > g.rows:
                x = jnp.concatenate([x, jnp.zeros((g.KX - g.rows, LANES), F32)], axis=0)
            for sh in range(3):
                if sh == 0:
                    moved = jnp.where(wide == 0, 0.0, pltpu.roll(x, 1, 1))
                elif sh == 2:
                    moved = jnp.where(wide == LANES - 1, 0.0, pltpu.roll(x, LANES - 1, 1))
                else:
                    moved = x
                moved = moved.astype(BF16)
                for r in range(3):
                    at = (ph * rows_h + chunk + 2 - r) * LANES
                    first = (r * 3 + sh) * g.KX
                    pat[first : first + g.KX, at : at + LANES] = moved

    def filters(n):
        at = LANES + n * wide_n
        patch = pat[:, at : at + wide_n]
        hid = jnp.maximum(dot(w1h[...], patch) + dot(w1l[...], patch), 0.0)
        hid_h, hid_l = split(hid)
        y[:, at : at + wide_n] = (
            dot(w2h[...], hid_h) + dot(w2l[...], hid_h) + dot(w2h[...], hid_l)
        )

    for ph in range(H2):
        taken(r1.at[ph], r_b1.at[ph])
        taken(r2.at[ph], r_b2.at[ph])
    wide_n = 2 * LANES
    done = 0
    for ph in range(H2):
        spread(ph)
        ready = g.HA if ph == H2 - 1 else (ph + 1) * rows_h - 1
        while (done + 1) * wide_n <= ready * LANES:
            filters(done)
            done += 1

    last = iota((g.unit, LANES), 1)
    for i in range(g.HA):
        sums = []
        for sh in range(3):
            part = None
            for r in range(3):
                first = (r * 3 + sh) * g.unit
                term = y[first : first + g.unit, (i + r) * LANES : (i + r + 1) * LANES]
                part = term if part is None else part + term
            sums.append(part)
        res = sums[1]
        res = res + jnp.where(last == 0, 0.0, pltpu.roll(sums[0], 1, 1))
        res = res + jnp.where(last == LANES - 1, 0.0, pltpu.roll(sums[2], LANES - 1, 1))
        for k in range(g.kb):
            for l in range(g.lb):
                n = k * g.lb + l
                out_ref[k, l, i : i + 1, :] = res[n : n + 1, :]

    taken(r2, s_b2.at[0])
    for ph, pt in peers:
        pltpu.make_async_copy(r1.at[0, 0], r1.at[0, 0], s_b1.at[0]).wait()


def per_device(feature_a, feature_b, conv_in, bias_in, conv_out):
    S, T = lax.axis_size("src"), lax.axis_size("tgt")
    g = Plan(S, T, feature_a.shape, feature_b.shape, conv_in.shape[0])
    s1 = jnp.asarray(g.select_in(), BF16)
    s2 = jnp.asarray(g.select_out(), BF16)
    vm = pl.BlockSpec(memory_space=pltpu.VMEM)
    hbm = pl.BlockSpec(memory_space=pl.ANY)
    dma = pltpu.SemaphoreType.DMA
    return pl.pallas_call(
        functools.partial(kernel, g),
        out_shape=jax.ShapeDtypeStruct((g.kb, g.lb, g.HA, g.WA), F32),
        in_specs=[hbm] * 7,
        out_specs=vm,
        scratch_shapes=[
            pltpu.VMEM((g.G,) + feature_a.shape, BF16),
            pltpu.VMEM(feature_b.shape, BF16),
            pltpu.VMEM(conv_in.shape, F32),
            pltpu.SMEM(bias_in.shape, F32),
            pltpu.VMEM(conv_out.shape, F32),
            pltpu.VMEM(s1.shape, BF16),
            pltpu.VMEM(s2.shape, BF16),
            dma((7,)),
            pltpu.VMEM((g.H2, T, g.kb, g.lb, g.C), BF16),
            pltpu.VMEM((g.H2, T * g.block, g.C), F32),
            pltpu.VMEM((g.H2, T * g.block, LANES), F32),
            pltpu.VMEM((g.H2 + 2, T + 2, g.block, LANES), BF16),
            pltpu.VMEM((g.H2, T, 1, g.bk, g.block, LANES), BF16),
            pltpu.VMEM((g.H2, T, 2, g.bk, g.block, LANES), BF16),
            pltpu.VMEM((g.H2, T, g.rows, LANES), F32),
            pltpu.VMEM((g.KP, (g.HA + 2) * LANES), BF16),
            pltpu.VMEM((g.M, g.KP), BF16),
            pltpu.VMEM((g.M, g.KP), BF16),
            pltpu.VMEM((g.Y, g.M), BF16),
            pltpu.VMEM((g.Y, g.M), BF16),
            pltpu.VMEM((g.Y, (g.HA + 2) * LANES), F32),
            pltpu.VMEM((g.hidden, LANES), F32),
            dma((1,)),
            dma((1,)),
            dma((1,)),
            dma((g.H2,)),
            dma((1,)),
            dma((1,)),
            dma((g.H2,)),
            dma((g.H2,)),
        ],
        compiler_params=pltpu.CompilerParams(
            collective_id=0, has_side_effects=True, vmem_limit_bytes=62 * 1024 * 1024
        ),
    )(feature_a, feature_b, conv_in, bias_in, conv_out, s1, s2)


def solution(mesh):
    in_specs = (P("src", "tgt", None), P("tgt", "src", None), P(), P(), P())
    out_specs = P("tgt", "src", None, None)
    return jax.shard_map(
        per_device, mesh=mesh, in_specs=in_specs, out_specs=out_specs, check_vma=False
    )
```

```python
import functools

import jax
import jax.numpy as jnp
import numpy as np
from jax import lax
from jax.experimental import pallas as pl
from jax.experimental.pallas import tpu as pltpu
from jax.sharding import PartitionSpec as P

LANES = 128
F32 = jnp.float32
BF16 = jnp.bfloat16


def round_up(value, unit):
    return -(-value // unit) * unit


class Plan:
    def __init__(self, count_s, count_t, a_shape, b_shape, hidden):
        self.S, self.T = count_s, count_t
        self.rows_i, self.cols_j, self.C = a_shape
        self.kb, self.lb = b_shape[0], b_shape[1]
        self.hidden = hidden
        self.G = 2
        assert count_s % self.G == 0
        self.H2 = count_s // self.G
        self.ij = self.rows_i * self.cols_j
        self.HA = self.rows_i * count_s
        self.WA = self.cols_j * count_t
        self.pair = self.G * self.ij
        assert self.WA == LANES and LANES % self.pair == 0 and self.kb >= 2 and self.lb >= 2
        self.bk = self.bl = 3
        self.block = self.kb * self.lb
        self.used = self.bk * self.bl * self.block
        self.rows = round_up(self.used + 1, 8)
        self.KX = round_up(self.rows, 16)
        self.KP = 9 * self.KX
        self.KW = round_up(self.KP, LANES)
        self.hk, self.hl = self.kb + 2, self.lb + 2
        self.M = self.hk * self.hl * 2 * hidden
        self.unit = round_up(self.block, 8)
        self.Y = round_up(9 * self.unit, 16)
        assert self.Y <= LANES

    def tap(self, net, p, q, r, s):
        p, q, r, s = (p, q, r, s) if net == 0 else (r, s, p, q)
        return 27 * p + 9 * q + 3 * r + s

    def select_in(self):
        out = np.zeros((LANES, self.kb, self.lb, 2, self.KW), np.float32)
        for k, l, net in np.ndindex(self.kb, self.lb, 2):
            for p, q, r, s in np.ndindex(3, 3, 3, 3):
                ek, el = k + p - 2 + self.kb, l + q - 2 + self.lb
                col = (r * 3 + s) * self.KX + (el % self.lb) + (ek % self.kb) * self.lb
                col += (el // self.lb * self.bk + ek // self.kb) * self.block
                out[self.tap(net, p, q, r, s), k, l, net, col] = 1
        return out.reshape(LANES, -1)

    def select_out(self):
        out = np.zeros((LANES, self.hk, self.hl, 2, LANES), np.float32)
        for k, l, net in np.ndindex(self.hk, self.hl, 2):
            for ok, ol, r, s in np.ndindex(self.kb, self.lb, 3, 3):
                p, q = k - ok, l - ol
                if 0 <= p < 3 and 0 <= q < 3:
                    col = (r * 3 + s) * self.unit + ok * self.lb + ol
                    out[self.tap(net, p, q, r, s), k, l, net, col] = 1
        return out.reshape(LANES, -1)


def split(x):
    high = x.astype(BF16)
    return high, (x - high.astype(F32)).astype(BF16)


def dot(x, y):
    return jnp.dot(x, y, preferred_element_type=F32)


def iota(shape, dim):
    return lax.broadcasted_iota(jnp.int32, shape, dim)


def kernel(
    g, a_hbm, b_hbm, cin_hbm, bias_hbm, cout_hbm, s1_hbm, s2_hbm, out_ref,
    ach, cin_ref, bias_ref, cout_ref, s1_vm, s2_vm, load_sem,
    bb, bf, vs, vp, r1, r2, u, pat, w1, w2, y, cpad,
    s_x, r_x, s_a, r_a, s_b1, s_b2, r_b1, r_b2,
):
    S, T = g.S, g.T
    H2 = g.H2
    N = H2 * T
    s = lax.axis_index("src")
    t = lax.axis_index("tgt")
    core = lax.rem(s, g.G)
    h = s // g.G
    sibling = s + 1 - 2 * core

    loads = [
        pltpu.make_async_copy(src, dst, load_sem.at[n])
        for n, (src, dst) in enumerate((
            (cin_hbm, cin_ref), (bias_hbm, bias_ref), (s1_hbm, s1_vm),
            (cout_hbm, cout_ref), (s2_hbm, s2_vm), (a_hbm, ach.at[core]),
        ))
    ]
    for load in loads:
        load.start()

    barrier = pltpu.get_barrier_semaphore()

    def greet(ps, pt):
        pl.semaphore_signal(
            barrier, inc=1, device_id={"src": ps, "tgt": pt}, device_id_type=pl.DeviceIdType.MESH
        )

    peers = [
        (lax.rem(h + n, H2), lax.rem(t + m, T)) for n in range(H2) for m in range(T) if n or m
    ]
    greet(sibling, t)
    for ph, pt in peers:
        greet(ph * g.G + core, pt)
    vp[...] = jnp.zeros(vp.shape, BF16)
    pl.semaphore_wait(barrier, N)

    def remote(src, dst, send, recv, ps, pt):
        return pltpu.make_async_remote_copy(
            src_ref=src, dst_ref=dst, send_sem=send, recv_sem=recv,
            device_id={"src": ps, "tgt": pt}, device_id_type=pl.DeviceIdType.MESH,
        )

    def taken(ref, sem):
        pltpu.make_async_copy(ref, ref, sem).wait()

    for ph, pt in peers:
        remote(b_hbm, bb.at[h, t], s_a.at[0], r_a.at[h], ph * g.G + core, pt).start()
    swap = remote(a_hbm, ach.at[core], s_x.at[0], r_x.at[0], sibling, t)
    swap.start()
    pltpu.make_async_copy(b_hbm, bb.at[h, t], r_a.at[h]).start()

    for load in loads[:3]:
        load.wait()
    cpad[...] = jnp.zeros(cpad.shape, F32)
    cpad[:, : cin_ref.shape[1]] = cin_ref[...]
    taps_h, taps_l = split(cpad[...])
    both = jnp.concatenate([taps_h.astype(F32), taps_l.astype(F32)], axis=0).astype(BF16)
    base = dot(both, s1_vm[...])
    H = g.hidden
    row = iota((H, LANES), 0)
    bias = jnp.zeros((H, LANES), F32)
    for n in range(H):
        bias = jnp.where(row == n, bias_ref[n], bias)
    bias_h, bias_l = (part.astype(F32) for part in split(bias))
    bias = jnp.concatenate([bias_h, bias_h, bias_l, bias_l], axis=0)
    bias = jnp.concatenate([bias] * (g.KW // LANES), axis=1)
    bias = jnp.where(iota(bias.shape, 1) == 4 * g.KX + g.rows - 1, bias, 0.0)
    for k in range(g.hk):
        at_k = t * g.kb + (k - 1)
        for l in range(g.hl):
            at_l = s * g.lb + (l - 1)
            parts = []
            for first in (0, H):
                for net in range(2):
                    at = ((k % g.kb * g.lb + l % g.lb) * 2 + net) * g.KW
                    parts.append(base[first : first + H, at : at + g.KW])
            block = jnp.concatenate(parts, axis=0)
            shift = (l // g.lb * g.bk + k // g.kb) * g.block
            if shift:
                block = pltpu.roll(block, shift, 1)
            inside = (at_k >= 0) & (at_k < T * g.kb) & (at_l >= 0) & (at_l < S * g.lb)
            block = (block + bias) * jnp.where(inside, 1.0, 0.0).astype(F32)
            at = (k * g.hl + l) * 2 * H
            w1[at : at + 2 * H, :] = block[: 2 * H, : g.KP].astype(BF16)
            w1[g.M + at : g.M + at + 2 * H, :] = block[2 * H :, : g.KP].astype(BF16)

    loads[3].wait()
    loads[4].wait()
    cpad[:, : cout_ref.shape[1]] = cout_ref[...]
    taps_h, taps_l = split(cpad[...])
    both = jnp.concatenate([taps_h.astype(F32), taps_l.astype(F32)], axis=0).astype(BF16)
    base = dot(both, s2_vm[...])
    blocks = g.hk * g.hl * 2
    for first, at in ((0, 0), (H, g.Y)):
        tall = jnp.concatenate(
            [base[first : first + H, n * LANES : (n + 1) * LANES] for n in range(blocks)], axis=0
        )
        w2[at : at + g.Y, :] = tall.T[: g.Y].astype(BF16)

    tail = g.rows - g.used
    u[:, :, g.used :, :] = jnp.where(
        iota((H2, T, tail, LANES), 2) == tail - 1, jnp.ones((H2, T, tail, LANES), F32), 0.0
    )
    pat[: 3 * g.KX, LANES : 2 * LANES] = jnp.zeros((3 * g.KX, LANES), BF16)
    pat[6 * g.KX :, g.HA * LANES : (g.HA + 1) * LANES] = jnp.zeros((3 * g.KX, LANES), BF16)
    y[:, :LANES] = jnp.zeros((g.Y, LANES), F32)
    y[:, (g.HA + 1) * LANES :] = jnp.zeros((g.Y, LANES), F32)

    loads[5].wait()
    swap.wait_recv()
    if g.pair == LANES:
        a = ach[...].reshape(g.pair, g.C)
    else:
        a = ach[...].astype(F32).reshape(g.pair, g.C)
        a = jnp.concatenate([a] * (LANES // g.pair), axis=0).astype(BF16)

    def near(ph, pt):
        return vp.at[pl.ds(ph + 1, 1), pl.ds(pt, g.bk)]

    def send_near(ph):
        for m in range(1, T):
            pt = lax.rem(t + m, T)
            remote(near(ph, pt), r1.at[h, t], s_b1.at[0], r_b1.at[h], ph * g.G + core, pt).start()

    def send_other(ph):
        for m in range(T):
            pt = lax.rem(t + m, T)
            remote(
                vp.at[pl.ds(ph + 1 - core, 2), pl.ds(pt, g.bk)], r2.at[h, t], s_b2.at[0],
                r_b2.at[h], ph * g.G + 1 - core, pt,
            ).start()

    for n in range(H2):
        ph = lax.rem(h + H2 - n, H2)
        taken(bb.at[ph], r_a.at[ph])
        for tt in range(T):
            for kk in range(g.kb):
                at = tt * g.block + kk * g.lb
                bf[n, at : at + g.lb, :] = bb[ph, tt, kk].astype(F32)
        vs[n] = lax.dot_general(
            bf[n].astype(BF16), a, (((1,), (1,)), ((), ())), preferred_element_type=F32
        ) * (g.C ** -0.5)
        for tt in range(T):
            vp[ph + 1, tt + 1] = vs[n, tt * g.block : (tt + 1) * g.block, :].astype(BF16)
        send_near(ph)
        if n:
            remote(
                near(ph, t), r1.at[h, t], s_b1.at[0], r_b1.at[h], ph * g.G + core, t
            ).start()
            send_other(lax.rem(h + H2 - n + core, H2))
        else:
            pltpu.make_async_copy(near(h, t), r1.at[h, t], r_b1.at[h]).start()
    send_other(lax.rem(h + core, H2))
    for ph, pt in peers:
        pltpu.make_async_copy(b_hbm, b_hbm, s_a.at[0]).wait()
    swap.wait_send()

    lane = iota((g.rows, LANES), 1)
    wide = iota((g.KX, LANES), 1)
    rows_h = g.G * g.rows_i

    def spread(ph):
        ins = []
        for tt in range(T):
            for dt in range(g.bk):
                for ds in range(g.bl):
                    at = (ds * g.bk + dt) * g.block
                    got = r1[ph, tt, 0, dt] if ds == 1 else r2[ph, tt, ds // 2, dt]
                    u[ph, tt, at : at + g.block, :] = got.astype(F32)
            ins.append(u[ph, tt])
        for chunk in range(rows_h):
            x = None
            for tt in range(T):
                shift = (tt - chunk) * g.cols_j % LANES
                moved = pltpu.roll(ins[tt], shift, 1) if shift else ins[tt]
                x = moved if tt == 0 else jnp.where(lane >= tt * g.cols_j, moved, x)
            if g.KX > g.rows:
                x = jnp.concatenate([x, jnp.zeros((g.KX - g.rows, LANES), F32)], axis=0)
            for sh in range(3):
                if sh == 0:
                    moved = jnp.where(wide == 0, 0.0, pltpu.roll(x, 1, 1))
                elif sh == 2:
                    moved = jnp.where(wide == LANES - 1, 0.0, pltpu.roll(x, LANES - 1, 1))
                else:
                    moved = x
                moved = moved.astype(BF16)
                for r in range(3):
                    at = (ph * rows_h + chunk + 2 - r) * LANES
                    first = (r * 3 + sh) * g.KX
                    pat[first : first + g.KX, at : at + LANES] = moved

    def filters(n):
        at = LANES + n * wide_n
        patch = pat[:, at : at + wide_n]
        hid = dot(w1[...], patch)
        hid_h, hid_l = split(jnp.maximum(hid[: g.M] + hid[g.M :], 0.0))
        res = dot(w2[...], hid_h)
        y[:, at : at + wide_n] = res[: g.Y] + res[g.Y :] + dot(w2[: g.Y, :], hid_l)

    for ph in range(H2):
        taken(r1.at[ph], r_b1.at[ph])
        taken(r2.at[ph], r_b2.at[ph])
    wide_n = 2 * LANES
    done = 0
    for ph in range(H2):
        spread(ph)
        ready = g.HA if ph == H2 - 1 else (ph + 1) * rows_h - 1
        while (done + 1) * wide_n <= ready * LANES:
            filters(done)
            done += 1

    last = iota((g.unit, LANES), 1)
    for i in range(g.HA):
        sums = []
        for sh in range(3):
            part = None
            for r in range(3):
                first = (r * 3 + sh) * g.unit
                term = y[first : first + g.unit, (i + r) * LANES : (i + r + 1) * LANES]
                part = term if part is None else part + term
            sums.append(part)
        res = sums[1]
        res = res + jnp.where(last == 0, 0.0, pltpu.roll(sums[0], 1, 1))
        res = res + jnp.where(last == LANES - 1, 0.0, pltpu.roll(sums[2], LANES - 1, 1))
        for k in range(g.kb):
            for l in range(g.lb):
                n = k * g.lb + l
                out_ref[k, l, i : i + 1, :] = res[n : n + 1, :]

    taken(r2, s_b2.at[0])
    for ph, pt in peers:
        pltpu.make_async_copy(r1.at[0, 0], r1.at[0, 0], s_b1.at[0]).wait()


def per_device(feature_a, feature_b, conv_in, bias_in, conv_out):
    S, T = lax.axis_size("src"), lax.axis_size("tgt")
    g = Plan(S, T, feature_a.shape, feature_b.shape, conv_in.shape[0])
    s1 = jnp.asarray(g.select_in(), BF16)
    s2 = jnp.asarray(g.select_out(), BF16)
    vm = pl.BlockSpec(memory_space=pltpu.VMEM)
    hbm = pl.BlockSpec(memory_space=pl.ANY)
    dma = pltpu.SemaphoreType.DMA
    return pl.pallas_call(
        functools.partial(kernel, g),
        out_shape=jax.ShapeDtypeStruct((g.kb, g.lb, g.HA, g.WA), F32),
        in_specs=[hbm] * 7,
        out_specs=vm,
        scratch_shapes=[
            pltpu.VMEM((g.G,) + feature_a.shape, BF16),
            pltpu.VMEM(conv_in.shape, F32),
            pltpu.SMEM(bias_in.shape, F32),
            pltpu.VMEM(conv_out.shape, F32),
            pltpu.VMEM(s1.shape, BF16),
            pltpu.VMEM(s2.shape, BF16),
            dma((6,)),
            pltpu.VMEM((g.H2, T, g.kb, g.lb, g.C), BF16),
            pltpu.VMEM((g.H2, T * g.block, g.C), F32),
            pltpu.VMEM((g.H2, T * g.block, LANES), F32),
            pltpu.VMEM((g.H2 + 2, T + 2, g.block, LANES), BF16),
            pltpu.VMEM((g.H2, T, 1, g.bk, g.block, LANES), BF16),
            pltpu.VMEM((g.H2, T, 2, g.bk, g.block, LANES), BF16),
            pltpu.VMEM((g.H2, T, g.rows, LANES), F32),
            pltpu.VMEM((g.KP, (g.HA + 2) * LANES), BF16),
            pltpu.VMEM((2 * g.M, g.KP), BF16),
            pltpu.VMEM((2 * g.Y, g.M), BF16),
            pltpu.VMEM((g.Y, (g.HA + 2) * LANES), F32),
            pltpu.VMEM((g.hidden, LANES), F32),
            dma((1,)),
            dma((1,)),
            dma((1,)),
            dma((g.H2,)),
            dma((1,)),
            dma((1,)),
            dma((g.H2,)),
            dma((g.H2,)),
        ],
        compiler_params=pltpu.CompilerParams(
            collective_id=0, has_side_effects=True, vmem_limit_bytes=62 * 1024 * 1024
        ),
    )(feature_a, feature_b, conv_in, bias_in, conv_out, s1, s2)


def solution(mesh):
    in_specs = (P("src", "tgt", None), P("tgt", "src", None), P(), P(), P())
    out_specs = P("tgt", "src", None, None)
    return jax.shard_map(
        per_device, mesh=mesh, in_specs=in_specs, out_specs=out_specs, check_vma=False
    )
```

```python
import functools

import jax
import jax.numpy as jnp
import numpy as np
from jax import lax
from jax.experimental import pallas as pl
from jax.experimental.pallas import tpu as pltpu
from jax.sharding import PartitionSpec as P

LANES = 128
F32 = jnp.float32
BF16 = jnp.bfloat16


def round_up(value, unit):
    return -(-value // unit) * unit


class Plan:
    def __init__(self, count_s, count_t, a_shape, b_shape, hidden):
        self.S, self.T = count_s, count_t
        self.rows_i, self.cols_j, self.C = a_shape
        self.kb, self.lb = b_shape[0], b_shape[1]
        self.hidden = hidden
        self.G = 2
        assert count_s % self.G == 0
        self.H2 = count_s // self.G
        self.ij = self.rows_i * self.cols_j
        self.HA = self.rows_i * count_s
        self.WA = self.cols_j * count_t
        self.pair = self.G * self.ij
        assert self.WA == LANES and LANES % self.pair == 0 and self.kb >= 2 and self.lb >= 2
        self.bk = self.bl = 3
        self.block = self.kb * self.lb
        self.used = self.bk * self.bl * self.block
        self.rows = round_up(self.used + 1, 8)
        self.KX = round_up(self.rows, 16)
        self.KP = 9 * self.KX
        self.KW = round_up(self.KP, LANES)
        self.hk, self.hl = self.kb + 2, self.lb + 2
        self.M = self.hk * self.hl * 2 * hidden
        self.unit = round_up(self.block, 8)
        self.Y = round_up(9 * self.unit, 16)
        assert self.Y <= LANES

    def tap(self, net, p, q, r, s):
        p, q, r, s = (p, q, r, s) if net == 0 else (r, s, p, q)
        return 27 * p + 9 * q + 3 * r + s

    def select_in(self):
        out = np.zeros((LANES, self.kb, self.lb, 2, self.KW), np.float32)
        for k, l, net in np.ndindex(self.kb, self.lb, 2):
            for p, q, r, s in np.ndindex(3, 3, 3, 3):
                ek, el = k + p - 2 + self.kb, l + q - 2 + self.lb
                col = (r * 3 + s) * self.KX + (el % self.lb) + (ek % self.kb) * self.lb
                col += (el // self.lb * self.bk + ek // self.kb) * self.block
                out[self.tap(net, p, q, r, s), k, l, net, col] = 1
        return out.reshape(LANES, -1)

    def select_out(self):
        out = np.zeros((LANES, self.hk, self.hl, 2, LANES), np.float32)
        for k, l, net in np.ndindex(self.hk, self.hl, 2):
            for ok, ol, r, s in np.ndindex(self.kb, self.lb, 3, 3):
                p, q = k - ok, l - ol
                if 0 <= p < 3 and 0 <= q < 3:
                    col = (r * 3 + s) * self.unit + ok * self.lb + ol
                    out[self.tap(net, p, q, r, s), k, l, net, col] = 1
        return out.reshape(LANES, -1)


def split(x):
    high = x.astype(BF16)
    return high, (x - high.astype(F32)).astype(BF16)


def dot(x, y):
    return jnp.dot(x, y, preferred_element_type=F32)


def iota(shape, dim):
    return lax.broadcasted_iota(jnp.int32, shape, dim)


def kernel(
    g, a_hbm, b_hbm, cin_hbm, bias_hbm, cout_hbm, s1_hbm, s2_hbm, out_ref,
    ach, cin_ref, bias_ref, cout_ref, s1_vm, s2_vm, load_sem,
    bb, bf, vs, vp, r1, r2, u, pat, w1, w2, y, cpad,
    s_x, r_x, s_a, r_a, s_b1, s_b2, r_b1, r_b2,
):
    S, T = g.S, g.T
    H2 = g.H2
    N = H2 * T
    s = lax.axis_index("src")
    t = lax.axis_index("tgt")
    core = lax.rem(s, g.G)
    h = s // g.G
    sibling = s + 1 - 2 * core

    loads = [
        pltpu.make_async_copy(src, dst, load_sem.at[n])
        for n, (src, dst) in enumerate((
            (cin_hbm, cin_ref), (bias_hbm, bias_ref), (s1_hbm, s1_vm),
            (cout_hbm, cout_ref), (s2_hbm, s2_vm), (a_hbm, ach.at[core]),
        ))
    ]
    for load in loads:
        load.start()

    barrier = pltpu.get_barrier_semaphore()

    def greet(ps, pt):
        pl.semaphore_signal(
            barrier, inc=1, device_id={"src": ps, "tgt": pt}, device_id_type=pl.DeviceIdType.MESH
        )

    peers = [
        (lax.rem(h + n, H2), lax.rem(t + m, T)) for n in range(H2) for m in range(T) if n or m
    ]
    greet(sibling, t)
    for ph, pt in peers:
        greet(ph * g.G + core, pt)
    vp[...] = jnp.zeros(vp.shape, BF16)
    pl.semaphore_wait(barrier, N)

    def remote(src, dst, send, recv, ps, pt):
        return pltpu.make_async_remote_copy(
            src_ref=src, dst_ref=dst, send_sem=send, recv_sem=recv,
            device_id={"src": ps, "tgt": pt}, device_id_type=pl.DeviceIdType.MESH,
        )

    def taken(ref, sem):
        pltpu.make_async_copy(ref, ref, sem).wait()

    for ph, pt in peers:
        remote(b_hbm, bb.at[h, t], s_a.at[0], r_a.at[h], ph * g.G + core, pt).start()
    swap = remote(a_hbm, ach.at[core], s_x.at[0], r_x.at[0], sibling, t)
    swap.start()
    pltpu.make_async_copy(b_hbm, bb.at[h, t], r_a.at[h]).start()

    for load in loads[:3]:
        load.wait()
    cpad[...] = jnp.zeros(cpad.shape, F32)
    cpad[:, : cin_ref.shape[1]] = cin_ref[...]
    taps_h, taps_l = split(cpad[...])
    both = jnp.concatenate([taps_h.astype(F32), taps_l.astype(F32)], axis=0).astype(BF16)
    base = dot(both, s1_vm[...])
    H = g.hidden
    row = iota((H, LANES), 0)
    bias = jnp.zeros((H, LANES), F32)
    for n in range(H):
        bias = jnp.where(row == n, bias_ref[n], bias)
    bias_h, bias_l = (part.astype(F32) for part in split(bias))
    bias = jnp.concatenate([bias_h, bias_h, bias_l, bias_l], axis=0)
    bias = jnp.concatenate([bias] * (g.KW // LANES), axis=1)
    bias = jnp.where(iota(bias.shape, 1) == 4 * g.KX + g.rows - 1, bias, 0.0)
    for k in range(g.hk):
        at_k = t * g.kb + (k - 1)
        for l in range(g.hl):
            at_l = s * g.lb + (l - 1)
            parts = []
            for first in (0, H):
                for net in range(2):
                    at = ((k % g.kb * g.lb + l % g.lb) * 2 + net) * g.KW
                    parts.append(base[first : first + H, at : at + g.KW])
            block = jnp.concatenate(parts, axis=0)
            shift = (l // g.lb * g.bk + k // g.kb) * g.block
            if shift:
                block = pltpu.roll(block, shift, 1)
            inside = (at_k >= 0) & (at_k < T * g.kb) & (at_l >= 0) & (at_l < S * g.lb)
            block = (block + bias) * jnp.where(inside, 1.0, 0.0).astype(F32)
            at = (k * g.hl + l) * 2 * H
            w1[at : at + 2 * H, :] = block[: 2 * H, : g.KP].astype(BF16)
            w1[g.M + at : g.M + at + 2 * H, :] = block[2 * H :, : g.KP].astype(BF16)

    loads[3].wait()
    loads[4].wait()
    cpad[:, : cout_ref.shape[1]] = cout_ref[...]
    taps_h, taps_l = split(cpad[...])
    both = jnp.concatenate([taps_h.astype(F32), taps_l.astype(F32)], axis=0).astype(BF16)
    base = dot(both, s2_vm[...])
    blocks = g.hk * g.hl * 2
    for first, at in ((0, 0), (H, g.Y)):
        tall = jnp.concatenate(
            [base[first : first + H, n * LANES : (n + 1) * LANES] for n in range(blocks)], axis=0
        )
        w2[at : at + g.Y, :] = tall.T[: g.Y].astype(BF16)

    tail = g.rows - g.used
    u[:, :, g.used :, :] = jnp.where(
        iota((H2, T, tail, LANES), 2) == tail - 1, jnp.ones((H2, T, tail, LANES), F32), 0.0
    )
    pat[: 3 * g.KX, LANES : 2 * LANES] = jnp.zeros((3 * g.KX, LANES), BF16)
    pat[6 * g.KX :, g.HA * LANES : (g.HA + 1) * LANES] = jnp.zeros((3 * g.KX, LANES), BF16)
    y[:, :LANES] = jnp.zeros((g.Y, LANES), F32)
    y[:, (g.HA + 1) * LANES :] = jnp.zeros((g.Y, LANES), F32)

    loads[5].wait()
    swap.wait_recv()
    if g.pair == LANES:
        a = ach[...].reshape(g.pair, g.C)
    else:
        a = ach[...].astype(F32).reshape(g.pair, g.C)
        a = jnp.concatenate([a] * (LANES // g.pair), axis=0).astype(BF16)

    def near(ph, pt):
        return vp.at[pl.ds(ph + 1, 1), pl.ds(pt, g.bk)]

    def send_near(ph):
        for m in range(1, T):
            pt = lax.rem(t + m, T)
            remote(near(ph, pt), r1.at[h, t], s_b1.at[0], r_b1.at[h], ph * g.G + core, pt).start()

    def send_other(ph):
        for m in range(T):
            pt = lax.rem(t + m, T)
            remote(
                vp.at[pl.ds(ph + 1 - core, 2), pl.ds(pt, g.bk)], r2.at[h, t], s_b2.at[0],
                r_b2.at[h], ph * g.G + 1 - core, pt,
            ).start()

    for n in range(H2):
        ph = lax.rem(h + H2 - n, H2)
        taken(bb.at[ph], r_a.at[ph])
        for tt in range(T):
            for kk in range(g.kb):
                at = tt * g.block + kk * g.lb
                bf[n, at : at + g.lb, :] = bb[ph, tt, kk].astype(F32)
        vs[n] = lax.dot_general(
            bf[n].astype(BF16), a, (((1,), (1,)), ((), ())), preferred_element_type=F32
        ) * (g.C ** -0.5)
        for tt in range(T):
            vp[ph + 1, tt + 1] = vs[n, tt * g.block : (tt + 1) * g.block, :].astype(BF16)
        send_near(ph)
        if n:
            remote(
                near(ph, t), r1.at[h, t], s_b1.at[0], r_b1.at[h], ph * g.G + core, t
            ).start()
            send_other(lax.rem(h + H2 - n + core, H2))
        else:
            pltpu.make_async_copy(near(h, t), r1.at[h, t], r_b1.at[h]).start()
    send_other(lax.rem(h + core, H2))
    for ph, pt in peers:
        pltpu.make_async_copy(b_hbm, b_hbm, s_a.at[0]).wait()
    swap.wait_send()

    lane = iota((g.rows, LANES), 1)
    wide = iota((g.KX, LANES), 1)
    rows_h = g.G * g.rows_i

    def spread(ph):
        ins = []
        for tt in range(T):
            for dt in range(g.bk):
                for ds in range(g.bl):
                    at = (ds * g.bk + dt) * g.block
                    got = r1[ph, tt, 0, dt] if ds == 1 else r2[ph, tt, ds // 2, dt]
                    u[ph, tt, at : at + g.block, :] = got.astype(F32)
            ins.append(u[ph, tt])
        for chunk in range(rows_h):
            x = None
            for tt in range(T):
                shift = (tt - chunk) * g.cols_j % LANES
                moved = pltpu.roll(ins[tt], shift, 1) if shift else ins[tt]
                x = moved if tt == 0 else jnp.where(lane >= tt * g.cols_j, moved, x)
            if g.KX > g.rows:
                x = jnp.concatenate([x, jnp.zeros((g.KX - g.rows, LANES), F32)], axis=0)
            for sh in range(3):
                if sh == 0:
                    moved = jnp.where(wide == 0, 0.0, pltpu.roll(x, 1, 1))
                elif sh == 2:
                    moved = jnp.where(wide == LANES - 1, 0.0, pltpu.roll(x, LANES - 1, 1))
                else:
                    moved = x
                moved = moved.astype(BF16)
                for r in range(3):
                    at = pl.multiple_of((ph * rows_h + chunk + 2 - r) * LANES, LANES)
                    first = (r * 3 + sh) * g.KX
                    pat[first : first + g.KX, pl.ds(at, LANES)] = moved

    def filters(rows):
        if not rows:
            return
        at = [pl.multiple_of((row + 1) * LANES, LANES) for row in rows]
        patch = jnp.concatenate([pat[:, pl.ds(place, LANES)] for place in at], axis=1)
        hid = dot(w1[...], patch)
        hid_h, hid_l = split(jnp.maximum(hid[: g.M] + hid[g.M :], 0.0))
        res = dot(w2[...], hid_h)
        res = res[: g.Y] + res[g.Y :] + dot(w2[: g.Y, :], hid_l)
        for n, place in enumerate(at):
            y[:, pl.ds(place, LANES)] = res[:, n * LANES : (n + 1) * LANES]

    def inner(ph):
        filters([ph * rows_h + n for n in range(1, rows_h - 1)])

    def between(ph):
        row = ph * rows_h + rows_h - 1
        filters([row, lax.rem(row + 1, g.HA)])

    order = [lax.rem(h + core + n, H2) for n in range(H2)]
    for n, ph in enumerate(order):
        taken(r1.at[ph], r_b1.at[ph])
        taken(r2.at[ph], r_b2.at[ph])
        if n >= 1:
            inner(order[n - 1])
        if n >= 2:
            between(order[n - 2])
        spread(ph)
    inner(order[-1])
    if H2 > 1:
        between(order[-2])
    between(order[-1])

    last = iota((g.unit, LANES), 1)
    for i in range(g.HA):
        sums = []
        for sh in range(3):
            part = None
            for r in range(3):
                first = (r * 3 + sh) * g.unit
                term = y[first : first + g.unit, (i + r) * LANES : (i + r + 1) * LANES]
                part = term if part is None else part + term
            sums.append(part)
        res = sums[1]
        res = res + jnp.where(last == 0, 0.0, pltpu.roll(sums[0], 1, 1))
        res = res + jnp.where(last == LANES - 1, 0.0, pltpu.roll(sums[2], LANES - 1, 1))
        for k in range(g.kb):
            for l in range(g.lb):
                n = k * g.lb + l
                out_ref[k, l, i : i + 1, :] = res[n : n + 1, :]

    taken(r2, s_b2.at[0])
    for ph, pt in peers:
        pltpu.make_async_copy(r1.at[0, 0], r1.at[0, 0], s_b1.at[0]).wait()


def per_device(feature_a, feature_b, conv_in, bias_in, conv_out):
    S, T = lax.axis_size("src"), lax.axis_size("tgt")
    g = Plan(S, T, feature_a.shape, feature_b.shape, conv_in.shape[0])
    s1 = jnp.asarray(g.select_in(), BF16)
    s2 = jnp.asarray(g.select_out(), BF16)
    vm = pl.BlockSpec(memory_space=pltpu.VMEM)
    hbm = pl.BlockSpec(memory_space=pl.ANY)
    dma = pltpu.SemaphoreType.DMA
    return pl.pallas_call(
        functools.partial(kernel, g),
        out_shape=jax.ShapeDtypeStruct((g.kb, g.lb, g.HA, g.WA), F32),
        in_specs=[hbm] * 7,
        out_specs=vm,
        scratch_shapes=[
            pltpu.VMEM((g.G,) + feature_a.shape, BF16),
            pltpu.VMEM(conv_in.shape, F32),
            pltpu.SMEM(bias_in.shape, F32),
            pltpu.VMEM(conv_out.shape, F32),
            pltpu.VMEM(s1.shape, BF16),
            pltpu.VMEM(s2.shape, BF16),
            dma((6,)),
            pltpu.VMEM((g.H2, T, g.kb, g.lb, g.C), BF16),
            pltpu.VMEM((g.H2, T * g.block, g.C), F32),
            pltpu.VMEM((g.H2, T * g.block, LANES), F32),
            pltpu.VMEM((g.H2 + 2, T + 2, g.block, LANES), BF16),
            pltpu.VMEM((g.H2, T, 1, g.bk, g.block, LANES), BF16),
            pltpu.VMEM((g.H2, T, 2, g.bk, g.block, LANES), BF16),
            pltpu.VMEM((g.H2, T, g.rows, LANES), F32),
            pltpu.VMEM((g.KP, (g.HA + 2) * LANES), BF16),
            pltpu.VMEM((2 * g.M, g.KP), BF16),
            pltpu.VMEM((2 * g.Y, g.M), BF16),
            pltpu.VMEM((g.Y, (g.HA + 2) * LANES), F32),
            pltpu.VMEM((g.hidden, LANES), F32),
            dma((1,)),
            dma((1,)),
            dma((1,)),
            dma((g.H2,)),
            dma((1,)),
            dma((1,)),
            dma((g.H2,)),
            dma((g.H2,)),
        ],
        compiler_params=pltpu.CompilerParams(
            collective_id=0, has_side_effects=True, vmem_limit_bytes=62 * 1024 * 1024
        ),
    )(feature_a, feature_b, conv_in, bias_in, conv_out, s1, s2)


def solution(mesh):
    in_specs = (P("src", "tgt", None), P("tgt", "src", None), P(), P(), P())
    out_specs = P("tgt", "src", None, None)
    return jax.shard_map(
        per_device, mesh=mesh, in_specs=in_specs, out_specs=out_specs, check_vma=False
    )
```

```python
import functools

import jax
import jax.numpy as jnp
import numpy as np
from jax import lax
from jax.experimental import pallas as pl
from jax.experimental.pallas import tpu as pltpu
from jax.sharding import PartitionSpec as P

LANES = 128
F32 = jnp.float32
BF16 = jnp.bfloat16


def round_up(value, unit):
    return -(-value // unit) * unit


class Plan:
    def __init__(self, count_s, count_t, a_shape, b_shape, hidden):
        self.S, self.T = count_s, count_t
        self.rows_i, self.cols_j, self.C = a_shape
        self.kb, self.lb = b_shape[0], b_shape[1]
        self.hidden = hidden
        self.G = 2
        assert count_s % self.G == 0 and count_t >= 2
        self.H2 = count_s // self.G
        self.ij = self.rows_i * self.cols_j
        self.HA = self.rows_i * count_s
        self.WA = self.cols_j * count_t
        self.pair = self.G * self.ij
        assert self.WA == LANES and LANES % self.pair == 0 and self.kb >= 2 and self.lb >= 2
        self.bk = self.bl = 3
        self.block = self.kb * self.lb
        self.used = self.bk * self.bl * self.block
        self.rows = round_up(self.used + 1, 8)
        self.KX = round_up(self.rows, 16)
        self.KP = 9 * self.KX
        self.KW = round_up(self.KP, LANES)
        self.hk, self.hl = self.kb + 2, self.lb + 2
        self.M = self.hk * self.hl * 2 * hidden
        self.unit = round_up(self.block, 8)
        self.Y = round_up(9 * self.unit, 16)
        assert self.Y <= LANES

    def tap(self, net, p, q, r, s):
        p, q, r, s = (p, q, r, s) if net == 0 else (r, s, p, q)
        return 27 * p + 9 * q + 3 * r + s

    def select_in(self):
        out = np.zeros((LANES, self.kb, self.lb, 2, self.KW), np.float32)
        for k, l, net in np.ndindex(self.kb, self.lb, 2):
            for p, q, r, s in np.ndindex(3, 3, 3, 3):
                ek, el = k + p - 2 + self.kb, l + q - 2 + self.lb
                col = (r * 3 + s) * self.KX + (el % self.lb) + (ek % self.kb) * self.lb
                col += (el // self.lb * self.bk + ek // self.kb) * self.block
                out[self.tap(net, p, q, r, s), k, l, net, col] = 1
        return out.reshape(LANES, -1)

    def select_out(self):
        out = np.zeros((LANES, self.hk, self.hl, 2, LANES), np.float32)
        for k, l, net in np.ndindex(self.hk, self.hl, 2):
            for ok, ol, r, s in np.ndindex(self.kb, self.lb, 3, 3):
                p, q = k - ok, l - ol
                if 0 <= p < 3 and 0 <= q < 3:
                    col = (r * 3 + s) * self.unit + ok * self.lb + ol
                    out[self.tap(net, p, q, r, s), k, l, net, col] = 1
        return out.reshape(LANES, -1)


def split(x):
    high = x.astype(BF16)
    return high, (x - high.astype(F32)).astype(BF16)


def dot(x, y):
    return jnp.dot(x, y, preferred_element_type=F32)


def iota(shape, dim):
    return lax.broadcasted_iota(jnp.int32, shape, dim)


def kernel(
    g, a_hbm, b_hbm, cin_hbm, bias_hbm, cout_hbm, s1_hbm, s2_hbm, out_ref,
    ach, cin_ref, bias_ref, cout_ref, s1_vm, s2_vm, load_sem,
    bb, bf, vs, vp, r1, r2, u, pat, w1, w2, y, cpad,
    s_x, r_x, s_a, r_a, s_b1, s_b2, r_b1, r_b2,
):
    S, T = g.S, g.T
    H2 = g.H2
    N = H2 * T
    s = lax.axis_index("src")
    t = lax.axis_index("tgt")
    core = lax.rem(s, g.G)
    h = s // g.G
    sibling = s + 1 - 2 * core

    barrier = pltpu.get_barrier_semaphore()

    def greet(ps, pt):
        pl.semaphore_signal(
            barrier, inc=1, device_id={"src": ps, "tgt": pt}, device_id_type=pl.DeviceIdType.MESH
        )

    peers = [
        (lax.rem(h + n, H2), lax.rem(t + m, T)) for n in range(H2) for m in range(T) if n or m
    ]
    greet(sibling, t)
    for ph, pt in peers:
        greet(ph * g.G + core, pt)
    loads = [
        pltpu.make_async_copy(src, dst, load_sem.at[n])
        for n, (src, dst) in enumerate((
            (cin_hbm, cin_ref), (bias_hbm, bias_ref), (s1_hbm, s1_vm),
            (cout_hbm, cout_ref), (s2_hbm, s2_vm), (a_hbm, ach.at[core]),
        ))
    ]
    for load in loads:
        load.start()

    vp[...] = jnp.zeros(vp.shape, BF16)
    pl.semaphore_wait(barrier, N)

    def remote(src, dst, send, recv, ps, pt):
        return pltpu.make_async_remote_copy(
            src_ref=src, dst_ref=dst, send_sem=send, recv_sem=recv,
            device_id={"src": ps, "tgt": pt}, device_id_type=pl.DeviceIdType.MESH,
        )

    def taken(ref, sem):
        pltpu.make_async_copy(ref, ref, sem).wait()

    for ph, pt in peers:
        remote(b_hbm, bb.at[h, t], s_a.at[0], r_a.at[h], ph * g.G + core, pt).start()
    swap = remote(a_hbm, ach.at[core], s_x.at[0], r_x.at[0], sibling, t)
    swap.start()
    pltpu.make_async_copy(b_hbm, bb.at[h, t], r_a.at[h]).start()

    for load in loads[:3]:
        load.wait()
    cpad[...] = jnp.zeros(cpad.shape, F32)
    cpad[:, : cin_ref.shape[1]] = cin_ref[...]
    taps_h, taps_l = split(cpad[...])
    both = jnp.concatenate([taps_h.astype(F32), taps_l.astype(F32)], axis=0).astype(BF16)
    base = dot(both, s1_vm[...])
    H = g.hidden
    row = iota((H, LANES), 0)
    bias = jnp.zeros((H, LANES), F32)
    for n in range(H):
        bias = jnp.where(row == n, bias_ref[n], bias)
    bias_h, bias_l = (part.astype(F32) for part in split(bias))
    bias = jnp.concatenate([bias_h, bias_h, bias_l, bias_l], axis=0)
    bias = jnp.concatenate([bias] * (g.KW // LANES), axis=1)
    bias = jnp.where(iota(bias.shape, 1) == 4 * g.KX + g.rows - 1, bias, 0.0)
    for k in range(g.hk):
        at_k = t * g.kb + (k - 1)
        for l in range(g.hl):
            at_l = s * g.lb + (l - 1)
            parts = []
            for first in (0, H):
                for net in range(2):
                    at = ((k % g.kb * g.lb + l % g.lb) * 2 + net) * g.KW
                    parts.append(base[first : first + H, at : at + g.KW])
            block = jnp.concatenate(parts, axis=0)
            shift = (l // g.lb * g.bk + k // g.kb) * g.block
            if shift:
                block = pltpu.roll(block, shift, 1)
            inside = (at_k >= 0) & (at_k < T * g.kb) & (at_l >= 0) & (at_l < S * g.lb)
            block = (block + bias) * jnp.where(inside, 1.0, 0.0).astype(F32)
            at = (k * g.hl + l) * 2 * H
            w1[at : at + 2 * H, :] = block[: 2 * H, : g.KP].astype(BF16)
            w1[g.M + at : g.M + at + 2 * H, :] = block[2 * H :, : g.KP].astype(BF16)

    loads[3].wait()
    loads[4].wait()
    cpad[:, : cout_ref.shape[1]] = cout_ref[...]
    taps_h, taps_l = split(cpad[...])
    both = jnp.concatenate([taps_h.astype(F32), taps_l.astype(F32)], axis=0).astype(BF16)
    base = dot(both, s2_vm[...])
    blocks = g.hk * g.hl * 2
    for first, at in ((0, 0), (H, g.Y)):
        tall = jnp.concatenate(
            [base[first : first + H, n * LANES : (n + 1) * LANES] for n in range(blocks)], axis=0
        )
        w2[at : at + g.Y, :] = tall.T[: g.Y].astype(BF16)

    tail = g.rows - g.used
    u[:, :, g.used :, :] = jnp.where(
        iota((H2, T, tail, LANES), 2) == tail - 1, jnp.ones((H2, T, tail, LANES), F32), 0.0
    )
    pat[: 3 * g.KX, LANES : 2 * LANES] = jnp.zeros((3 * g.KX, LANES), BF16)
    pat[6 * g.KX :, g.HA * LANES : (g.HA + 1) * LANES] = jnp.zeros((3 * g.KX, LANES), BF16)
    y[:, :LANES] = jnp.zeros((g.Y, LANES), F32)
    y[:, (g.HA + 1) * LANES :] = jnp.zeros((g.Y, LANES), F32)

    loads[5].wait()
    swap.wait_recv()
    if g.pair == LANES:
        a = ach[...].reshape(g.pair, g.C)
    else:
        a = ach[...].astype(F32).reshape(g.pair, g.C)
        a = jnp.concatenate([a] * (LANES // g.pair), axis=0).astype(BF16)

    reach = [slice(1 if pt == 0 else 0, g.bk - 1 if pt == T - 1 else g.bk) for pt in range(T)]
    rows_t = sorted(range(T), key=lambda pt: min(pt, T - 1 - pt))
    at_edge = (t == 0) | (t == T - 1)

    @pl.when(t == 0)
    def _():
        r1[:, :, :, 0] = jnp.zeros((H2, T, 1, g.block, LANES), BF16)
        r2[:, :, :, 0] = jnp.zeros((H2, T, 2, g.block, LANES), BF16)

    @pl.when(t == T - 1)
    def _():
        r1[:, :, :, g.bk - 1] = jnp.zeros((H2, T, 1, g.block, LANES), BF16)
        r2[:, :, :, g.bk - 1] = jnp.zeros((H2, T, 2, g.block, LANES), BF16)

    def source(first, count, pt):
        return vp.at[pl.ds(first, count), pt + reach[pt].start : pt + reach[pt].stop]

    def near(ph, pt):
        return remote(
            source(ph + 1, 1, pt), r1.at[h, t, :, reach[pt]], s_b1.at[0], r_b1.at[h],
            ph * g.G + core, pt,
        )

    def send_other(ph):
        for pt in rows_t:
            remote(
                source(ph + 1 - core, 2, pt), r2.at[h, t, :, reach[pt]], s_b2.at[0], r_b2.at[h],
                ph * g.G + 1 - core, pt,
            ).start()

    for n in range(H2):
        ph = lax.rem(h + H2 - n, H2)
        taken(bb.at[ph], r_a.at[ph])
        for tt in range(T):
            for kk in range(g.kb):
                at = tt * g.block + kk * g.lb
                bf[n, at : at + g.lb, :] = bb[ph, tt, kk].astype(F32)
        vs[n] = lax.dot_general(
            bf[n].astype(BF16), a, (((1,), (1,)), ((), ())), preferred_element_type=F32
        ) * (g.C ** -0.5)
        for tt in range(T):
            vp[ph + 1, tt + 1] = vs[n, tt * g.block : (tt + 1) * g.block, :].astype(BF16)
        for pt in rows_t:
            if n:
                near(ph, pt).start()
                continue

            @pl.when(t != pt)
            def _():
                near(ph, pt).start()

            @pl.when(t == pt)
            def _():
                pltpu.make_async_copy(
                    source(h + 1, 1, pt), r1.at[h, t, :, reach[pt]], r_b1.at[h]
                ).start()

        if n:
            send_other(lax.rem(h + H2 - n + core, H2))
    send_other(lax.rem(h + core, H2))
    for ph, pt in peers:
        pltpu.make_async_copy(b_hbm, b_hbm, s_a.at[0]).wait()
    swap.wait_send()

    lane = iota((g.rows, LANES), 1)
    wide = iota((g.KX, LANES), 1)
    rows_h = g.G * g.rows_i

    def spread(ph):
        ins = []
        for tt in range(T):
            for dt in range(g.bk):
                for ds in range(g.bl):
                    at = (ds * g.bk + dt) * g.block
                    got = r1[ph, tt, 0, dt] if ds == 1 else r2[ph, tt, ds // 2, dt]
                    u[ph, tt, at : at + g.block, :] = got.astype(F32)
            ins.append(u[ph, tt])
        for chunk in range(rows_h):
            x = None
            for tt in range(T):
                shift = (tt - chunk) * g.cols_j % LANES
                moved = pltpu.roll(ins[tt], shift, 1) if shift else ins[tt]
                x = moved if tt == 0 else jnp.where(lane >= tt * g.cols_j, moved, x)
            if g.KX > g.rows:
                x = jnp.concatenate([x, jnp.zeros((g.KX - g.rows, LANES), F32)], axis=0)
            for sh in range(3):
                if sh == 0:
                    moved = jnp.where(wide == 0, 0.0, pltpu.roll(x, 1, 1))
                elif sh == 2:
                    moved = jnp.where(wide == LANES - 1, 0.0, pltpu.roll(x, LANES - 1, 1))
                else:
                    moved = x
                moved = moved.astype(BF16)
                for r in range(3):
                    at = pl.multiple_of((ph * rows_h + chunk + 2 - r) * LANES, LANES)
                    first = (r * 3 + sh) * g.KX
                    pat[first : first + g.KX, pl.ds(at, LANES)] = moved

    def filters(rows):
        if not rows:
            return
        at = [pl.multiple_of((row + 1) * LANES, LANES) for row in rows]
        patch = jnp.concatenate([pat[:, pl.ds(place, LANES)] for place in at], axis=1)
        hid = dot(w1[...], patch)
        hid_h, hid_l = split(jnp.maximum(hid[: g.M] + hid[g.M :], 0.0))
        res = dot(w2[...], hid_h)
        res = res[: g.Y] + res[g.Y :] + dot(w2[: g.Y, :], hid_l)
        for n, place in enumerate(at):
            y[:, pl.ds(place, LANES)] = res[:, n * LANES : (n + 1) * LANES]

    def inner(ph):
        filters([ph * rows_h + n for n in range(1, rows_h - 1)])

    def between(ph):
        row = ph * rows_h + rows_h - 1
        filters([row, lax.rem(row + 1, g.HA)])

    last = iota((g.unit, LANES), 1)

    def finish(ph):
        for n in range(rows_h):
            i = ph * rows_h + n
            sums = []
            for sh in range(3):
                part = None
                for r in range(3):
                    first = (r * 3 + sh) * g.unit
                    at = pl.multiple_of((i + r) * LANES, LANES)
                    term = y[first : first + g.unit, pl.ds(at, LANES)]
                    part = term if part is None else part + term
                sums.append(part)
            res = sums[1]
            res = res + jnp.where(last == 0, 0.0, pltpu.roll(sums[0], 1, 1))
            res = res + jnp.where(last == LANES - 1, 0.0, pltpu.roll(sums[2], LANES - 1, 1))
            for k in range(g.kb):
                for l in range(g.lb):
                    m = k * g.lb + l
                    out_ref[k, l, pl.ds(i, 1), :] = res[m : m + 1, :]

    order = [lax.rem(h + core + n, H2) for n in range(H2)]
    edge = slice(0, g.bk - 1)
    for n, ph in enumerate(order):

        @pl.when(at_edge)
        def _():
            taken(r1.at[ph, :, :, edge], r_b1.at[ph])
            taken(r2.at[ph, :, :, edge], r_b2.at[ph])

        @pl.when(jnp.logical_not(at_edge))
        def _():
            taken(r1.at[ph], r_b1.at[ph])
            taken(r2.at[ph], r_b2.at[ph])

        if n >= 1:
            inner(order[n - 1])
        if n >= 2:
            between(order[n - 2])
        if n >= 3:
            finish(order[n - 2])
        spread(ph)
    inner(order[-1])
    if H2 > 1:
        between(order[-2])
    between(order[-1])
    for n in range(H2):
        if n == 0 or n >= max(H2 - 2, 1):
            finish(order[n])

    taken(r2.at[:, 1 : T - 1], s_b2.at[0])
    taken(r2.at[:, :2, :, edge], s_b2.at[0])
    for n in range(H2):
        for pt in range(T):
            part = r1.at[0, 0, :, reach[pt]]
            if n:
                taken(part, s_b1.at[0])
                continue

            @pl.when(t != pt)
            def _():
                taken(part, s_b1.at[0])


def per_device(feature_a, feature_b, conv_in, bias_in, conv_out):
    S, T = lax.axis_size("src"), lax.axis_size("tgt")
    g = Plan(S, T, feature_a.shape, feature_b.shape, conv_in.shape[0])
    s1 = jnp.asarray(g.select_in(), BF16)
    s2 = jnp.asarray(g.select_out(), BF16)
    vm = pl.BlockSpec(memory_space=pltpu.VMEM)
    hbm = pl.BlockSpec(memory_space=pl.ANY)
    dma = pltpu.SemaphoreType.DMA
    return pl.pallas_call(
        functools.partial(kernel, g),
        out_shape=jax.ShapeDtypeStruct((g.kb, g.lb, g.HA, g.WA), F32),
        in_specs=[hbm] * 7,
        out_specs=vm,
        scratch_shapes=[
            pltpu.VMEM((g.G,) + feature_a.shape, BF16),
            pltpu.VMEM(conv_in.shape, F32),
            pltpu.SMEM(bias_in.shape, F32),
            pltpu.VMEM(conv_out.shape, F32),
            pltpu.VMEM(s1.shape, BF16),
            pltpu.VMEM(s2.shape, BF16),
            dma((6,)),
            pltpu.VMEM((g.H2, T, g.kb, g.lb, g.C), BF16),
            pltpu.VMEM((g.H2, T * g.block, g.C), F32),
            pltpu.VMEM((g.H2, T * g.block, LANES), F32),
            pltpu.VMEM((g.H2 + 2, T + 2, g.block, LANES), BF16),
            pltpu.VMEM((g.H2, T, 1, g.bk, g.block, LANES), BF16),
            pltpu.VMEM((g.H2, T, 2, g.bk, g.block, LANES), BF16),
            pltpu.VMEM((g.H2, T, g.rows, LANES), F32),
            pltpu.VMEM((g.KP, (g.HA + 2) * LANES), BF16),
            pltpu.VMEM((2 * g.M, g.KP), BF16),
            pltpu.VMEM((2 * g.Y, g.M), BF16),
            pltpu.VMEM((g.Y, (g.HA + 2) * LANES), F32),
            pltpu.VMEM((g.hidden, LANES), F32),
            dma((1,)),
            dma((1,)),
            dma((1,)),
            dma((g.H2,)),
            dma((1,)),
            dma((1,)),
            dma((g.H2,)),
            dma((g.H2,)),
        ],
        compiler_params=pltpu.CompilerParams(
            collective_id=0, has_side_effects=True, vmem_limit_bytes=62 * 1024 * 1024
        ),
    )(feature_a, feature_b, conv_in, bias_in, conv_out, s1, s2)


def solution(mesh):
    in_specs = (P("src", "tgt", None), P("tgt", "src", None), P(), P(), P())
    out_specs = P("tgt", "src", None, None)
    return jax.shard_map(
        per_device, mesh=mesh, in_specs=in_specs, out_specs=out_specs, check_vma=False
    )
```

```python
import functools

import jax
import jax.numpy as jnp
import numpy as np
from jax import lax
from jax.experimental import pallas as pl
from jax.experimental.pallas import tpu as pltpu
from jax.sharding import PartitionSpec as P

LANES = 128
F32 = jnp.float32
BF16 = jnp.bfloat16


def round_up(value, unit):
    return -(-value // unit) * unit


class Plan:
    def __init__(self, count_s, count_t, a_shape, b_shape, hidden):
        self.S, self.T = count_s, count_t
        self.rows_i, self.cols_j, self.C = a_shape
        self.kb, self.lb = b_shape[0], b_shape[1]
        self.hidden = hidden
        self.G = 2
        assert count_s % self.G == 0 and count_t >= 2
        self.H2 = count_s // self.G
        self.ij = self.rows_i * self.cols_j
        self.HA = self.rows_i * count_s
        self.WA = self.cols_j * count_t
        self.pair = self.G * self.ij
        assert self.WA == LANES and LANES % self.pair == 0 and self.kb >= 2 and self.lb >= 2
        self.bk = self.bl = 3
        self.block = self.kb * self.lb
        self.used = self.bk * self.bl * self.block
        self.rows = round_up(self.used + 1, 8)
        self.KX = round_up(self.rows, 16)
        self.KP = 9 * self.KX
        self.KW = round_up(self.KP, LANES)
        self.hk, self.hl = self.kb + 2, self.lb + 2
        self.M = self.hk * self.hl * 2 * hidden
        self.unit = round_up(self.block, 8)
        self.Y = round_up(9 * self.unit, 16)
        assert self.Y <= LANES

    def tap(self, net, p, q, r, s):
        p, q, r, s = (p, q, r, s) if net == 0 else (r, s, p, q)
        return 27 * p + 9 * q + 3 * r + s

    def select_in(self):
        out = np.zeros((LANES, self.kb, self.lb, 2, self.KW), np.float32)
        for k, l, net in np.ndindex(self.kb, self.lb, 2):
            for p, q, r, s in np.ndindex(3, 3, 3, 3):
                ek, el = k + p - 2 + self.kb, l + q - 2 + self.lb
                col = (r * 3 + s) * self.KX + (el % self.lb) + (ek % self.kb) * self.lb
                col += (el // self.lb * self.bk + ek // self.kb) * self.block
                out[self.tap(net, p, q, r, s), k, l, net, col] = 1
        return out.reshape(LANES, -1)

    def select_out(self):
        out = np.zeros((LANES, self.hk, self.hl, 2, LANES), np.float32)
        for k, l, net in np.ndindex(self.hk, self.hl, 2):
            for ok, ol, r, s in np.ndindex(self.kb, self.lb, 3, 3):
                p, q = k - ok, l - ol
                if 0 <= p < 3 and 0 <= q < 3:
                    col = (r * 3 + s) * self.unit + ok * self.lb + ol
                    out[self.tap(net, p, q, r, s), k, l, net, col] = 1
        return out.reshape(LANES, -1)


def split(x):
    high = x.astype(BF16)
    return high, (x - high.astype(F32)).astype(BF16)


def dot(x, y):
    return jnp.dot(x, y, preferred_element_type=F32)


def iota(shape, dim):
    return lax.broadcasted_iota(jnp.int32, shape, dim)


def kernel(
    g, a_hbm, b_hbm, cin_hbm, bias_hbm, cout_hbm, s1_hbm, s2_hbm, out_ref,
    ach, cin_ref, bias_ref, cout_ref, s1_vm, s2_vm, load_sem,
    bb, bf, vs, vp, r1, r2, u, pat, w1, w2, y, cpad,
    s_x, r_x, s_a, r_a, s_b1, s_b2, r_b1, r_b2,
):
    S, T = g.S, g.T
    H2 = g.H2
    N = H2 * T
    s = lax.axis_index("src")
    t = lax.axis_index("tgt")
    core = lax.rem(s, g.G)
    h = s // g.G
    sibling = s + 1 - 2 * core

    barrier = pltpu.get_barrier_semaphore()

    def greet(ps, pt):
        pl.semaphore_signal(
            barrier, inc=1, device_id={"src": ps, "tgt": pt}, device_id_type=pl.DeviceIdType.MESH
        )

    peers = [
        (lax.rem(h + n, H2), lax.rem(t + m, T)) for n in range(H2) for m in range(T) if n or m
    ]
    greet(sibling, t)
    for ph, pt in peers:
        greet(ph * g.G + core, pt)
    loads = [
        pltpu.make_async_copy(src, dst, load_sem.at[n])
        for n, (src, dst) in enumerate((
            (cin_hbm, cin_ref), (bias_hbm, bias_ref), (s1_hbm, s1_vm),
            (cout_hbm, cout_ref), (s2_hbm, s2_vm), (a_hbm, ach.at[core]),
        ))
    ]
    for load in loads:
        load.start()

    vp[...] = jnp.zeros(vp.shape, BF16)
    pl.semaphore_wait(barrier, N)

    def remote(src, dst, send, recv, ps, pt):
        return pltpu.make_async_remote_copy(
            src_ref=src, dst_ref=dst, send_sem=send, recv_sem=recv,
            device_id={"src": ps, "tgt": pt}, device_id_type=pl.DeviceIdType.MESH,
        )

    def taken(ref, sem):
        pltpu.make_async_copy(ref, ref, sem).wait()

    for ph, pt in peers:
        remote(b_hbm, bb.at[h, t], s_a.at[0], r_a.at[h], ph * g.G + core, pt).start()
    swap = remote(a_hbm, ach.at[core], s_x.at[0], r_x.at[0], sibling, t)
    swap.start()
    pltpu.make_async_copy(b_hbm, bb.at[h, t], r_a.at[h]).start()

    for load in loads[:3]:
        load.wait()
    cpad[...] = jnp.zeros(cpad.shape, F32)
    cpad[:, : cin_ref.shape[1]] = cin_ref[...]
    taps_h, taps_l = split(cpad[...])
    both = jnp.concatenate([taps_h.astype(F32), taps_l.astype(F32)], axis=0).astype(BF16)
    base = dot(both, s1_vm[...])
    H = g.hidden
    row = iota((H, LANES), 0)
    bias = jnp.zeros((H, LANES), F32)
    for n in range(H):
        bias = jnp.where(row == n, bias_ref[n], bias)
    bias_h, bias_l = (part.astype(F32) for part in split(bias))
    bias = jnp.concatenate([bias_h, bias_h, bias_l, bias_l], axis=0)
    bias = jnp.concatenate([bias] * (g.KW // LANES), axis=1)
    bias = jnp.where(iota(bias.shape, 1) == 4 * g.KX + g.rows - 1, bias, 0.0)
    for k in range(g.hk):
        at_k = t * g.kb + (k - 1)
        for l in range(g.hl):
            at_l = s * g.lb + (l - 1)
            parts = []
            for first in (0, H):
                for net in range(2):
                    at = ((k % g.kb * g.lb + l % g.lb) * 2 + net) * g.KW
                    parts.append(base[first : first + H, at : at + g.KW])
            block = jnp.concatenate(parts, axis=0)
            shift = (l // g.lb * g.bk + k // g.kb) * g.block
            if shift:
                block = pltpu.roll(block, shift, 1)
            inside = (at_k >= 0) & (at_k < T * g.kb) & (at_l >= 0) & (at_l < S * g.lb)
            block = (block + bias) * jnp.where(inside, 1.0, 0.0).astype(F32)
            at = (k * g.hl + l) * 2 * H
            w1[at : at + 2 * H, :] = block[: 2 * H].astype(BF16)
            w1[g.M + at : g.M + at + 2 * H, :] = block[2 * H :].astype(BF16)

    tail = g.rows - g.used
    u[:, :, g.used :, :] = jnp.where(
        iota((H2, T, tail, LANES), 2) == tail - 1, jnp.ones((H2, T, tail, LANES), F32), 0.0
    )
    pat[: 3 * g.KX, LANES : 2 * LANES] = jnp.zeros((3 * g.KX, LANES), BF16)
    if g.KW > g.KP:
        pat[g.KP :, :] = jnp.zeros((g.KW - g.KP, (g.HA + 2) * LANES), BF16)
    pat[6 * g.KX : g.KP, g.HA * LANES : (g.HA + 1) * LANES] = jnp.zeros((3 * g.KX, LANES), BF16)
    y[:, :LANES] = jnp.zeros((g.Y, LANES), F32)
    y[:, (g.HA + 1) * LANES :] = jnp.zeros((g.Y, LANES), F32)

    loads[5].wait()
    swap.wait_recv()
    if g.pair == LANES:
        a = ach[...].reshape(g.pair, g.C)
    else:
        a = ach[...].astype(F32).reshape(g.pair, g.C)
        a = jnp.concatenate([a] * (LANES // g.pair), axis=0).astype(BF16)

    reach = [slice(1 if pt == 0 else 0, g.bk - 1 if pt == T - 1 else g.bk) for pt in range(T)]
    rows_t = sorted(range(T), key=lambda pt: min(pt, T - 1 - pt))
    at_edge = (t == 0) | (t == T - 1)

    @pl.when(t == 0)
    def _():
        r1[:, :, :, 0] = jnp.zeros((H2, T, 1, g.block, LANES), BF16)
        r2[:, :, :, 0] = jnp.zeros((H2, T, 2, g.block, LANES), BF16)

    @pl.when(t == T - 1)
    def _():
        r1[:, :, :, g.bk - 1] = jnp.zeros((H2, T, 1, g.block, LANES), BF16)
        r2[:, :, :, g.bk - 1] = jnp.zeros((H2, T, 2, g.block, LANES), BF16)

    def source(first, count, pt):
        return vp.at[pl.ds(first, count), pt + reach[pt].start : pt + reach[pt].stop]

    def near(ph, pt):
        return remote(
            source(ph + 1, 1, pt), r1.at[h, t, :, reach[pt]], s_b1.at[0], r_b1.at[h],
            ph * g.G + core, pt,
        )

    def send_other(ph):
        for pt in rows_t:
            remote(
                source(ph + 1 - core, 2, pt), r2.at[h, t, :, reach[pt]], s_b2.at[0], r_b2.at[h],
                ph * g.G + 1 - core, pt,
            ).start()

    def columns(steps):
        rows = T * g.block
        for n in steps:
            ph = lax.rem(h + H2 - n, H2)
            taken(bb.at[ph], r_a.at[ph])
            for tt in range(T):
                for kk in range(g.kb):
                    at = tt * g.block + kk * g.lb
                    bf[n, at : at + g.lb, :] = bb[ph, tt, kk].astype(F32)
        first, count = steps[0], len(steps)
        targets = bf[first : first + count].reshape(count * rows, g.C).astype(BF16)
        scores = lax.dot_general(
            targets, a, (((1,), (1,)), ((), ())), preferred_element_type=F32
        ) * (g.C ** -0.5)
        vs[first : first + count] = scores.reshape(count, rows, LANES)
        for n in steps:
            ph = lax.rem(h + H2 - n, H2)
            for tt in range(T):
                vp[ph + 1, tt + 1] = vs[n, tt * g.block : (tt + 1) * g.block, :].astype(BF16)
        for n in steps:
            ph = lax.rem(h + H2 - n, H2)
            for pt in rows_t:
                if n:
                    near(ph, pt).start()
                    continue

                @pl.when(t != pt)
                def _():
                    near(ph, pt).start()

                @pl.when(t == pt)
                def _():
                    pltpu.make_async_copy(
                        source(h + 1, 1, pt), r1.at[h, t, :, reach[pt]], r_b1.at[h]
                    ).start()

            if n:
                send_other(lax.rem(h + H2 - n + core, H2))

    half = -(-H2 // 2)
    columns(range(half))
    if half < H2:
        columns(range(half, H2))
    send_other(lax.rem(h + core, H2))

    loads[3].wait()
    loads[4].wait()
    cpad[:, : cout_ref.shape[1]] = cout_ref[...]
    taps_h, taps_l = split(cpad[...])
    both = jnp.concatenate([taps_h.astype(F32), taps_l.astype(F32)], axis=0).astype(BF16)
    base = dot(both, s2_vm[...])
    blocks = g.hk * g.hl * 2
    for first, at in ((0, 0), (H, g.Y)):
        tall = jnp.concatenate(
            [base[first : first + H, n * LANES : (n + 1) * LANES] for n in range(blocks)], axis=0
        )
        w2[at : at + g.Y, :] = tall.T[: g.Y].astype(BF16)

    for ph, pt in peers:
        pltpu.make_async_copy(b_hbm, b_hbm, s_a.at[0]).wait()
    swap.wait_send()

    lane = iota((g.rows, LANES), 1)
    wide = iota((g.KX, LANES), 1)
    rows_h = g.G * g.rows_i

    def spread(ph):
        ins = []
        for tt in range(T):
            for dt in range(g.bk):
                for ds in range(g.bl):
                    at = (ds * g.bk + dt) * g.block
                    got = r1[ph, tt, 0, dt] if ds == 1 else r2[ph, tt, ds // 2, dt]
                    u[ph, tt, at : at + g.block, :] = got.astype(F32)
            ins.append(u[ph, tt])
        for chunk in range(rows_h):
            x = None
            for tt in range(T):
                shift = (tt - chunk) * g.cols_j % LANES
                moved = pltpu.roll(ins[tt], shift, 1) if shift else ins[tt]
                x = moved if tt == 0 else jnp.where(lane >= tt * g.cols_j, moved, x)
            if g.KX > g.rows:
                x = jnp.concatenate([x, jnp.zeros((g.KX - g.rows, LANES), F32)], axis=0)
            for sh in range(3):
                if sh == 0:
                    moved = jnp.where(wide == 0, 0.0, pltpu.roll(x, 1, 1))
                elif sh == 2:
                    moved = jnp.where(wide == LANES - 1, 0.0, pltpu.roll(x, LANES - 1, 1))
                else:
                    moved = x
                moved = moved.astype(BF16)
                for r in range(3):
                    at = pl.multiple_of((ph * rows_h + chunk + 2 - r) * LANES, LANES)
                    first = (r * 3 + sh) * g.KX
                    pat[first : first + g.KX, pl.ds(at, LANES)] = moved

    def filters(rows):
        if not rows:
            return
        at = [pl.multiple_of((row + 1) * LANES, LANES) for row in rows]
        patch = jnp.concatenate([pat[:, pl.ds(place, LANES)] for place in at], axis=1)
        hid = dot(w1[...], patch)
        hid_h, hid_l = split(jnp.maximum(hid[: g.M] + hid[g.M :], 0.0))
        res = dot(w2[...], hid_h)
        res = res[: g.Y] + res[g.Y :] + dot(w2[: g.Y, :], hid_l)
        for n, place in enumerate(at):
            y[:, pl.ds(place, LANES)] = res[:, n * LANES : (n + 1) * LANES]

    def inner(ph):
        filters([ph * rows_h + n for n in range(1, rows_h - 1)])

    def between(ph):
        row = ph * rows_h + rows_h - 1
        filters([row, lax.rem(row + 1, g.HA)])

    last = iota((g.unit, LANES), 1)

    def finish(ph):
        for n in range(rows_h):
            i = ph * rows_h + n
            sums = []
            for sh in range(3):
                part = None
                for r in range(3):
                    first = (r * 3 + sh) * g.unit
                    at = pl.multiple_of((i + r) * LANES, LANES)
                    term = y[first : first + g.unit, pl.ds(at, LANES)]
                    part = term if part is None else part + term
                sums.append(part)
            res = sums[1]
            res = res + jnp.where(last == 0, 0.0, pltpu.roll(sums[0], 1, 1))
            res = res + jnp.where(last == LANES - 1, 0.0, pltpu.roll(sums[2], LANES - 1, 1))
            for k in range(g.kb):
                for l in range(g.lb):
                    m = k * g.lb + l
                    out_ref[k, l, pl.ds(i, 1), :] = res[m : m + 1, :]

    order = [lax.rem(h + core + n, H2) for n in range(H2)]
    edge = slice(0, g.bk - 1)
    for n, ph in enumerate(order):

        @pl.when(at_edge)
        def _():
            taken(r1.at[ph, :, :, edge], r_b1.at[ph])
            taken(r2.at[ph, :, :, edge], r_b2.at[ph])

        @pl.when(jnp.logical_not(at_edge))
        def _():
            taken(r1.at[ph], r_b1.at[ph])
            taken(r2.at[ph], r_b2.at[ph])

        if n >= 1:
            inner(order[n - 1])
        if n >= 2:
            between(order[n - 2])
        if n >= 3:
            finish(order[n - 2])
        spread(ph)
    inner(order[-1])
    if H2 > 1:
        between(order[-2])
    between(order[-1])
    for n in range(H2):
        if n == 0 or n >= max(H2 - 2, 1):
            finish(order[n])

    taken(r2.at[:, 1 : T - 1], s_b2.at[0])
    taken(r2.at[:, :2, :, edge], s_b2.at[0])
    for n in range(H2):
        for pt in range(T):
            part = r1.at[0, 0, :, reach[pt]]
            if n:
                taken(part, s_b1.at[0])
                continue

            @pl.when(t != pt)
            def _():
                taken(part, s_b1.at[0])


def per_device(feature_a, feature_b, conv_in, bias_in, conv_out):
    S, T = lax.axis_size("src"), lax.axis_size("tgt")
    g = Plan(S, T, feature_a.shape, feature_b.shape, conv_in.shape[0])
    s1 = jnp.asarray(g.select_in(), BF16)
    s2 = jnp.asarray(g.select_out(), BF16)
    vm = pl.BlockSpec(memory_space=pltpu.VMEM)
    hbm = pl.BlockSpec(memory_space=pl.ANY)
    dma = pltpu.SemaphoreType.DMA
    return pl.pallas_call(
        functools.partial(kernel, g),
        out_shape=jax.ShapeDtypeStruct((g.kb, g.lb, g.HA, g.WA), F32),
        in_specs=[hbm] * 7,
        out_specs=vm,
        scratch_shapes=[
            pltpu.VMEM((g.G,) + feature_a.shape, BF16),
            pltpu.VMEM(conv_in.shape, F32),
            pltpu.SMEM(bias_in.shape, F32),
            pltpu.VMEM(conv_out.shape, F32),
            pltpu.VMEM(s1.shape, BF16),
            pltpu.VMEM(s2.shape, BF16),
            dma((6,)),
            pltpu.VMEM((g.H2, T, g.kb, g.lb, g.C), BF16),
            pltpu.VMEM((g.H2, T * g.block, g.C), F32),
            pltpu.VMEM((g.H2, T * g.block, LANES), F32),
            pltpu.VMEM((g.H2 + 2, T + 2, g.block, LANES), BF16),
            pltpu.VMEM((g.H2, T, 1, g.bk, g.block, LANES), BF16),
            pltpu.VMEM((g.H2, T, 2, g.bk, g.block, LANES), BF16),
            pltpu.VMEM((g.H2, T, g.rows, LANES), F32),
            pltpu.VMEM((g.KW, (g.HA + 2) * LANES), BF16),
            pltpu.VMEM((2 * g.M, g.KW), BF16),
            pltpu.VMEM((2 * g.Y, g.M), BF16),
            pltpu.VMEM((g.Y, (g.HA + 2) * LANES), F32),
            pltpu.VMEM((g.hidden, LANES), F32),
            dma((1,)),
            dma((1,)),
            dma((1,)),
            dma((g.H2,)),
            dma((1,)),
            dma((1,)),
            dma((g.H2,)),
            dma((g.H2,)),
        ],
        compiler_params=pltpu.CompilerParams(
            collective_id=0, has_side_effects=True, vmem_limit_bytes=62 * 1024 * 1024
        ),
    )(feature_a, feature_b, conv_in, bias_in, conv_out, s1, s2)


def solution(mesh):
    in_specs = (P("src", "tgt", None), P("tgt", "src", None), P(), P(), P())
    out_specs = P("tgt", "src", None, None)
    return jax.shard_map(
        per_device, mesh=mesh, in_specs=in_specs, out_specs=out_specs, check_vma=False
    )
```

```python
import functools

import jax
import jax.numpy as jnp
import numpy as np
from jax import lax
from jax.experimental import pallas as pl
from jax.experimental.pallas import tpu as pltpu
from jax.sharding import PartitionSpec as P

LANES = 128
F32 = jnp.float32
BF16 = jnp.bfloat16


def round_up(value, unit):
    return -(-value // unit) * unit


class Plan:
    def __init__(self, count_s, count_t, a_shape, b_shape, hidden):
        self.S, self.T = count_s, count_t
        self.rows_i, self.cols_j, self.C = a_shape
        self.kb, self.lb = b_shape[0], b_shape[1]
        self.hidden = hidden
        self.G = 2
        assert count_s % self.G == 0 and count_t >= 2
        self.H2 = count_s // self.G
        self.ij = self.rows_i * self.cols_j
        self.HA = self.rows_i * count_s
        self.WA = self.cols_j * count_t
        self.pair = self.G * self.ij
        assert self.WA == LANES and LANES % self.pair == 0 and self.kb >= 2 and self.lb >= 2
        self.bk = self.bl = 3
        self.block = self.kb * self.lb
        self.used = self.bk * self.bl * self.block
        self.rows = round_up(self.used + 1, 8)
        self.KX = round_up(self.rows, 16)
        self.KP = 9 * self.KX
        self.KW = round_up(self.KP, LANES)
        self.hk, self.hl = self.kb + 2, self.lb + 2
        self.M = self.hk * self.hl * 2 * hidden
        self.unit = round_up(self.block, 8)
        self.Y = round_up(9 * self.unit, 16)
        assert self.Y <= LANES

    def tap(self, net, p, q, r, s):
        p, q, r, s = (p, q, r, s) if net == 0 else (r, s, p, q)
        return 27 * p + 9 * q + 3 * r + s

    def select_in(self):
        out = np.zeros((LANES, self.kb, self.lb, 2, self.KW), np.float32)
        for k, l, net in np.ndindex(self.kb, self.lb, 2):
            for p, q, r, s in np.ndindex(3, 3, 3, 3):
                ek, el = k + p - 2 + self.kb, l + q - 2 + self.lb
                col = (r * 3 + s) * self.KX + (el % self.lb) + (ek % self.kb) * self.lb
                col += (el // self.lb * self.bk + ek // self.kb) * self.block
                out[self.tap(net, p, q, r, s), k, l, net, col] = 1
        return out.reshape(LANES, -1)

    def select_out(self):
        out = np.zeros((LANES, self.hk, self.hl, 2, LANES), np.float32)
        for k, l, net in np.ndindex(self.hk, self.hl, 2):
            for ok, ol, r, s in np.ndindex(self.kb, self.lb, 3, 3):
                p, q = k - ok, l - ol
                if 0 <= p < 3 and 0 <= q < 3:
                    col = (r * 3 + s) * self.unit + ok * self.lb + ol
                    out[self.tap(net, p, q, r, s), k, l, net, col] = 1
        return out.reshape(LANES, -1)


def split(x):
    high = x.astype(BF16)
    return high, (x - high.astype(F32)).astype(BF16)


def dot(x, y):
    return jnp.dot(x, y, preferred_element_type=F32)


def iota(shape, dim):
    return lax.broadcasted_iota(jnp.int32, shape, dim)


def kernel(
    g, a_hbm, b_hbm, cin_hbm, bias_hbm, cout_hbm, s1_hbm, s2_hbm, out_ref,
    ach, cin_ref, bias_ref, cout_ref, s1_vm, s2_vm, load_sem,
    bb, bf, vs, vp, r1, r2, u, pat, w1, w2, y, cpad,
    s_x, r_x, s_a, r_a, s_b1, s_b2, r_b1, r_b2,
):
    S, T = g.S, g.T
    H2 = g.H2
    N = H2 * T
    s = lax.axis_index("src")
    t = lax.axis_index("tgt")
    core = lax.rem(s, g.G)
    h = s // g.G
    sibling = s + 1 - 2 * core

    barrier = pltpu.get_barrier_semaphore()

    def greet(ps, pt):
        pl.semaphore_signal(
            barrier, inc=1, device_id={"src": ps, "tgt": pt}, device_id_type=pl.DeviceIdType.MESH
        )

    peers = [
        (lax.rem(h + n, H2), lax.rem(t + m, T)) for n in range(H2) for m in range(T) if n or m
    ]
    greet(sibling, t)
    for ph, pt in peers:
        greet(ph * g.G + core, pt)
    loads = [
        pltpu.make_async_copy(src, dst, load_sem.at[n])
        for n, (src, dst) in enumerate((
            (cin_hbm, cin_ref), (bias_hbm, bias_ref), (s1_hbm, s1_vm),
            (cout_hbm, cout_ref), (s2_hbm, s2_vm), (a_hbm, ach.at[core]),
        ))
    ]
    for load in loads:
        load.start()

    vp[...] = jnp.zeros(vp.shape, BF16)
    pl.semaphore_wait(barrier, N)

    def remote(src, dst, send, recv, ps, pt):
        return pltpu.make_async_remote_copy(
            src_ref=src, dst_ref=dst, send_sem=send, recv_sem=recv,
            device_id={"src": ps, "tgt": pt}, device_id_type=pl.DeviceIdType.MESH,
        )

    def taken(ref, sem):
        pltpu.make_async_copy(ref, ref, sem).wait()

    for ph, pt in peers:
        remote(b_hbm, bb.at[h, t], s_a.at[0], r_a.at[h], ph * g.G + core, pt).start()
    swap = remote(a_hbm, ach.at[core], s_x.at[0], r_x.at[0], sibling, t)
    swap.start()
    pltpu.make_async_copy(b_hbm, bb.at[h, t], r_a.at[h]).start()

    for load in loads[:3]:
        load.wait()
    cpad[...] = jnp.zeros(cpad.shape, F32)
    cpad[:, : cin_ref.shape[1]] = cin_ref[...]
    taps_h, taps_l = split(cpad[...])
    both = jnp.concatenate([taps_h.astype(F32), taps_l.astype(F32)], axis=0).astype(BF16)
    base = dot(both, s1_vm[...])
    H = g.hidden
    row = iota((H, LANES), 0)
    bias = jnp.zeros((H, LANES), F32)
    for n in range(H):
        bias = jnp.where(row == n, bias_ref[n], bias)
    bias_h, bias_l = (part.astype(F32) for part in split(bias))
    bias = jnp.concatenate([bias_h, bias_h, bias_l, bias_l], axis=0)
    bias = jnp.concatenate([bias] * (g.KW // LANES), axis=1)
    bias = jnp.where(iota(bias.shape, 1) == 4 * g.KX + g.rows - 1, bias, 0.0)
    for k in range(g.hk):
        at_k = t * g.kb + (k - 1)
        for l in range(g.hl):
            at_l = s * g.lb + (l - 1)
            parts = []
            for first in (0, H):
                for net in range(2):
                    at = ((k % g.kb * g.lb + l % g.lb) * 2 + net) * g.KW
                    parts.append(base[first : first + H, at : at + g.KW])
            block = jnp.concatenate(parts, axis=0)
            shift = (l // g.lb * g.bk + k // g.kb) * g.block
            if shift:
                block = pltpu.roll(block, shift, 1)
            inside = (at_k >= 0) & (at_k < T * g.kb) & (at_l >= 0) & (at_l < S * g.lb)
            block = (block + bias) * jnp.where(inside, 1.0, 0.0).astype(F32)
            at = (k * g.hl + l) * 2 * H
            w1[at : at + 2 * H, :] = block[: 2 * H, : g.KP].astype(BF16)
            w1[g.M + at : g.M + at + 2 * H, :] = block[2 * H :, : g.KP].astype(BF16)

    loads[3].wait()
    loads[4].wait()
    cpad[:, : cout_ref.shape[1]] = cout_ref[...]
    taps_h, taps_l = split(cpad[...])
    both = jnp.concatenate([taps_h.astype(F32), taps_l.astype(F32)], axis=0).astype(BF16)
    base = dot(both, s2_vm[...])
    blocks = g.hk * g.hl * 2
    for first, at in ((0, 0), (H, g.Y)):
        tall = jnp.concatenate(
            [base[first : first + H, n * LANES : (n + 1) * LANES] for n in range(blocks)], axis=0
        )
        w2[at : at + g.Y, :] = tall.T[: g.Y].astype(BF16)

    tail = g.rows - g.used
    u[:, :, g.used :, :] = jnp.where(
        iota((H2, T, tail, LANES), 2) == tail - 1, jnp.ones((H2, T, tail, LANES), F32), 0.0
    )
    pat[: 3 * g.KX, LANES : 2 * LANES] = jnp.zeros((3 * g.KX, LANES), BF16)
    pat[6 * g.KX :, g.HA * LANES : (g.HA + 1) * LANES] = jnp.zeros((3 * g.KX, LANES), BF16)
    y[:, :LANES] = jnp.zeros((g.Y, LANES), F32)
    y[:, (g.HA + 1) * LANES :] = jnp.zeros((g.Y, LANES), F32)

    loads[5].wait()
    swap.wait_recv()
    if g.pair == LANES:
        a = ach[...].reshape(g.pair, g.C)
    else:
        a = ach[...].astype(F32).reshape(g.pair, g.C)
        a = jnp.concatenate([a] * (LANES // g.pair), axis=0).astype(BF16)

    reach = [slice(1 if pt == 0 else 0, g.bk - 1 if pt == T - 1 else g.bk) for pt in range(T)]
    rows_t = sorted(range(T), key=lambda pt: min(pt, T - 1 - pt))
    at_edge = (t == 0) | (t == T - 1)

    @pl.when(t == 0)
    def _():
        r1[:, :, :, 0] = jnp.zeros((H2, T, 1, g.block, LANES), BF16)
        r2[:, :, :, 0] = jnp.zeros((H2, T, 2, g.block, LANES), BF16)

    @pl.when(t == T - 1)
    def _():
        r1[:, :, :, g.bk - 1] = jnp.zeros((H2, T, 1, g.block, LANES), BF16)
        r2[:, :, :, g.bk - 1] = jnp.zeros((H2, T, 2, g.block, LANES), BF16)

    def source(first, count, pt):
        return vp.at[pl.ds(first, count), pt + reach[pt].start : pt + reach[pt].stop]

    def near(ph, pt):
        return remote(
            source(ph + 1, 1, pt), r1.at[h, t, :, reach[pt]], s_b1.at[0], r_b1.at[h],
            ph * g.G + core, pt,
        )

    def send_other(ph):
        for pt in rows_t:
            remote(
                source(ph + 1 - core, 2, pt), r2.at[h, t, :, reach[pt]], s_b2.at[0], r_b2.at[h],
                ph * g.G + 1 - core, pt,
            ).start()

    for n in range(H2):
        ph = lax.rem(h + H2 - n, H2)
        taken(bb.at[ph], r_a.at[ph])
        for tt in range(T):
            for kk in range(g.kb):
                at = tt * g.block + kk * g.lb
                bf[n, at : at + g.lb, :] = bb[ph, tt, kk].astype(F32)
        vs[n] = lax.dot_general(
            bf[n].astype(BF16), a, (((1,), (1,)), ((), ())), preferred_element_type=F32
        ) * (g.C ** -0.5)
        for tt in range(T):
            vp[ph + 1, tt + 1] = vs[n, tt * g.block : (tt + 1) * g.block, :].astype(BF16)
        for pt in rows_t:
            if n:
                near(ph, pt).start()
                continue

            @pl.when(t != pt)
            def _():
                near(ph, pt).start()

            @pl.when(t == pt)
            def _():
                pltpu.make_async_copy(
                    source(h + 1, 1, pt), r1.at[h, t, :, reach[pt]], r_b1.at[h]
                ).start()

        if n:
            send_other(lax.rem(h + H2 - n + core, H2))
    send_other(lax.rem(h + core, H2))
    for ph, pt in peers:
        pltpu.make_async_copy(b_hbm, b_hbm, s_a.at[0]).wait()
    swap.wait_send()

    lane = iota((g.rows, LANES), 1)
    wide = iota((g.KX, LANES), 1)
    rows_h = g.G * g.rows_i

    def spread(ph):
        ins = []
        for tt in range(T):
            for dt in range(g.bk):
                for ds in range(g.bl):
                    at = (ds * g.bk + dt) * g.block
                    got = r1[ph, tt, 0, dt] if ds == 1 else r2[ph, tt, ds // 2, dt]
                    u[ph, tt, at : at + g.block, :] = got.astype(F32)
            ins.append(u[ph, tt])
        for chunk in range(rows_h):
            x = None
            for tt in range(T):
                shift = (tt - chunk) * g.cols_j % LANES
                moved = pltpu.roll(ins[tt], shift, 1) if shift else ins[tt]
                x = moved if tt == 0 else jnp.where(lane >= tt * g.cols_j, moved, x)
            if g.KX > g.rows:
                x = jnp.concatenate([x, jnp.zeros((g.KX - g.rows, LANES), F32)], axis=0)
            for sh in range(3):
                if sh == 0:
                    moved = jnp.where(wide == 0, 0.0, pltpu.roll(x, 1, 1))
                elif sh == 2:
                    moved = jnp.where(wide == LANES - 1, 0.0, pltpu.roll(x, LANES - 1, 1))
                else:
                    moved = x
                moved = moved.astype(BF16)
                for r in range(3):
                    at = pl.multiple_of((ph * rows_h + chunk + 2 - r) * LANES, LANES)
                    first = (r * 3 + sh) * g.KX
                    pat[first : first + g.KX, pl.ds(at, LANES)] = moved

    def filters(rows):
        if not rows:
            return
        at = [pl.multiple_of((row + 1) * LANES, LANES) for row in rows]
        patch = jnp.concatenate([pat[:, pl.ds(place, LANES)] for place in at], axis=1)
        hid = dot(w1[...], patch)
        hid_h, hid_l = split(jnp.maximum(hid[: g.M] + hid[g.M :], 0.0))
        res = dot(w2[...], hid_h)
        res = res[: g.Y] + res[g.Y :] + dot(w2[: g.Y, :], hid_l)
        for n, place in enumerate(at):
            y[:, pl.ds(place, LANES)] = res[:, n * LANES : (n + 1) * LANES]

    def inner(ph):
        filters([ph * rows_h + n for n in range(1, rows_h - 1)])

    def between(ph):
        row = ph * rows_h + rows_h - 1
        filters([row, lax.rem(row + 1, g.HA)])

    last = iota((g.unit, LANES), 1)

    def finish(ph):
        for n in range(rows_h):
            i = ph * rows_h + n
            sums = []
            for sh in range(3):
                part = None
                for r in range(3):
                    first = (r * 3 + sh) * g.unit
                    at = pl.multiple_of((i + r) * LANES, LANES)
                    term = y[first : first + g.unit, pl.ds(at, LANES)]
                    part = term if part is None else part + term
                sums.append(part)
            res = sums[1]
            res = res + jnp.where(last == 0, 0.0, pltpu.roll(sums[0], 1, 1))
            res = res + jnp.where(last == LANES - 1, 0.0, pltpu.roll(sums[2], LANES - 1, 1))
            for k in range(g.kb):
                for l in range(g.lb):
                    m = k * g.lb + l
                    out_ref[k, l, pl.ds(i, 1), :] = res[m : m + 1, :]

    order = [lax.rem(h + n, H2) for n in range(H2)]
    edge = slice(0, g.bk - 1)
    for n, ph in enumerate(order):

        @pl.when(at_edge)
        def _():
            taken(r1.at[ph, :, :, edge], r_b1.at[ph])
            taken(r2.at[ph, :, :, edge], r_b2.at[ph])

        @pl.when(jnp.logical_not(at_edge))
        def _():
            taken(r1.at[ph], r_b1.at[ph])
            taken(r2.at[ph], r_b2.at[ph])

        if n >= 1:
            inner(order[n - 1])
        if n >= 2:
            between(order[n - 2])
        if n >= 3:
            finish(order[n - 2])
        spread(ph)
    inner(order[-1])
    if H2 > 1:
        between(order[-2])
    between(order[-1])
    for n in range(H2):
        if n == 0 or n >= max(H2 - 2, 1):
            finish(order[n])

    taken(r2.at[:, 1 : T - 1], s_b2.at[0])
    taken(r2.at[:, :2, :, edge], s_b2.at[0])
    for n in range(H2):
        for pt in range(T):
            part = r1.at[0, 0, :, reach[pt]]
            if n:
                taken(part, s_b1.at[0])
                continue

            @pl.when(t != pt)
            def _():
                taken(part, s_b1.at[0])


def per_device(feature_a, feature_b, conv_in, bias_in, conv_out):
    S, T = lax.axis_size("src"), lax.axis_size("tgt")
    g = Plan(S, T, feature_a.shape, feature_b.shape, conv_in.shape[0])
    s1 = jnp.asarray(g.select_in(), BF16)
    s2 = jnp.asarray(g.select_out(), BF16)
    vm = pl.BlockSpec(memory_space=pltpu.VMEM)
    hbm = pl.BlockSpec(memory_space=pl.ANY)
    dma = pltpu.SemaphoreType.DMA
    return pl.pallas_call(
        functools.partial(kernel, g),
        out_shape=jax.ShapeDtypeStruct((g.kb, g.lb, g.HA, g.WA), F32),
        in_specs=[hbm] * 7,
        out_specs=vm,
        scratch_shapes=[
            pltpu.VMEM((g.G,) + feature_a.shape, BF16),
            pltpu.VMEM(conv_in.shape, F32),
            pltpu.SMEM(bias_in.shape, F32),
            pltpu.VMEM(conv_out.shape, F32),
            pltpu.VMEM(s1.shape, BF16),
            pltpu.VMEM(s2.shape, BF16),
            dma((6,)),
            pltpu.VMEM((g.H2, T, g.kb, g.lb, g.C), BF16),
            pltpu.VMEM((g.H2, T * g.block, g.C), F32),
            pltpu.VMEM((g.H2, T * g.block, LANES), F32),
            pltpu.VMEM((g.H2 + 2, T + 2, g.block, LANES), BF16),
            pltpu.VMEM((g.H2, T, 1, g.bk, g.block, LANES), BF16),
            pltpu.VMEM((g.H2, T, 2, g.bk, g.block, LANES), BF16),
            pltpu.VMEM((g.H2, T, g.rows, LANES), F32),
            pltpu.VMEM((g.KP, (g.HA + 2) * LANES), BF16),
            pltpu.VMEM((2 * g.M, g.KP), BF16),
            pltpu.VMEM((2 * g.Y, g.M), BF16),
            pltpu.VMEM((g.Y, (g.HA + 2) * LANES), F32),
            pltpu.VMEM((g.hidden, LANES), F32),
            dma((1,)),
            dma((1,)),
            dma((1,)),
            dma((g.H2,)),
            dma((1,)),
            dma((1,)),
            dma((g.H2,)),
            dma((g.H2,)),
        ],
        compiler_params=pltpu.CompilerParams(
            collective_id=0, has_side_effects=True, vmem_limit_bytes=62 * 1024 * 1024
        ),
    )(feature_a, feature_b, conv_in, bias_in, conv_out, s1, s2)


def solution(mesh):
    in_specs = (P("src", "tgt", None), P("tgt", "src", None), P(), P(), P())
    out_specs = P("tgt", "src", None, None)
    return jax.shard_map(
        per_device, mesh=mesh, in_specs=in_specs, out_specs=out_specs, check_vma=False
    )
```

```python
import functools

import jax
import jax.numpy as jnp
import numpy as np
from jax import lax
from jax.experimental import pallas as pl
from jax.experimental.pallas import tpu as pltpu
from jax.sharding import PartitionSpec as P

LANES = 128
F32 = jnp.float32
BF16 = jnp.bfloat16


def round_up(value, unit):
    return -(-value // unit) * unit


class Plan:
    def __init__(self, count_s, count_t, a_shape, b_shape, hidden):
        self.S, self.T = count_s, count_t
        self.rows_i, self.cols_j, self.C = a_shape
        self.kb, self.lb = b_shape[0], b_shape[1]
        self.hidden = hidden
        self.G = 2
        assert count_s % self.G == 0 and count_t >= 2
        self.H2 = count_s // self.G
        self.ij = self.rows_i * self.cols_j
        self.HA = self.rows_i * count_s
        self.WA = self.cols_j * count_t
        self.pair = self.G * self.ij
        assert self.WA == LANES and LANES % self.pair == 0 and self.kb >= 2 and self.lb >= 2
        self.bk = self.bl = 3
        self.block = self.kb * self.lb
        self.used = self.bk * self.bl * self.block
        self.rows = round_up(self.used + 1, 8)
        self.KX = round_up(self.rows, 16)
        self.KP = 9 * self.KX
        self.KW = round_up(self.KP, LANES)
        self.hk, self.hl = self.kb + 2, self.lb + 2
        self.M = self.hk * self.hl * 2 * hidden
        self.unit = round_up(self.block, 8)
        self.Y = round_up(9 * self.unit, 16)
        assert self.Y <= LANES

    def tap(self, net, p, q, r, s):
        p, q, r, s = (p, q, r, s) if net == 0 else (r, s, p, q)
        return 27 * p + 9 * q + 3 * r + s

    def select_in(self):
        out = np.zeros((LANES, self.kb, self.lb, 2, self.KW), np.float32)
        for k, l, net in np.ndindex(self.kb, self.lb, 2):
            for p, q, r, s in np.ndindex(3, 3, 3, 3):
                ek, el = k + p - 2 + self.kb, l + q - 2 + self.lb
                col = (r * 3 + s) * self.KX + (el % self.lb) + (ek % self.kb) * self.lb
                col += (el // self.lb * self.bk + ek // self.kb) * self.block
                out[self.tap(net, p, q, r, s), k, l, net, col] = 1
        return out.reshape(LANES, -1)

    def select_out(self):
        out = np.zeros((LANES, self.hk, self.hl, 2, LANES), np.float32)
        for k, l, net in np.ndindex(self.hk, self.hl, 2):
            for ok, ol, r, s in np.ndindex(self.kb, self.lb, 3, 3):
                p, q = k - ok, l - ol
                if 0 <= p < 3 and 0 <= q < 3:
                    col = (r * 3 + s) * self.unit + ok * self.lb + ol
                    out[self.tap(net, p, q, r, s), k, l, net, col] = 1
        return out.reshape(LANES, -1)


def split(x):
    high = x.astype(BF16)
    return high, (x - high.astype(F32)).astype(BF16)


def dot(x, y):
    return jnp.dot(x, y, preferred_element_type=F32)


def iota(shape, dim):
    return lax.broadcasted_iota(jnp.int32, shape, dim)


def kernel(
    g, a_hbm, b_hbm, cin_hbm, bias_hbm, cout_hbm, s1_hbm, s2_hbm, out_ref,
    ach, cin_ref, bias_ref, cout_ref, s1_vm, s2_vm, load_sem,
    bb, bf, vs, vp, r1, r2, u, pat, w1, w2, y, cpad,
    s_x, r_x, s_a, r_a, s_b1, s_b2, r_b1, r_b2,
):
    S, T = g.S, g.T
    H2 = g.H2
    N = H2 * T
    s = lax.axis_index("src")
    t = lax.axis_index("tgt")
    core = lax.rem(s, g.G)
    h = s // g.G
    sibling = s + 1 - 2 * core

    barrier = pltpu.get_barrier_semaphore()

    def greet(ps, pt):
        pl.semaphore_signal(
            barrier, inc=1, device_id={"src": ps, "tgt": pt}, device_id_type=pl.DeviceIdType.MESH
        )

    peers = [
        (lax.rem(h + n, H2), lax.rem(t + m, T)) for n in range(H2) for m in range(T) if n or m
    ]
    greet(sibling, t)
    for ph, pt in peers:
        greet(ph * g.G + core, pt)
    loads = [
        pltpu.make_async_copy(src, dst, load_sem.at[n])
        for n, (src, dst) in enumerate((
            (cin_hbm, cin_ref), (bias_hbm, bias_ref), (s1_hbm, s1_vm),
            (cout_hbm, cout_ref), (s2_hbm, s2_vm), (a_hbm, ach.at[core]),
        ))
    ]
    for load in loads:
        load.start()

    vp[...] = jnp.zeros(vp.shape, BF16)
    pl.semaphore_wait(barrier, N)

    def remote(src, dst, send, recv, ps, pt):
        return pltpu.make_async_remote_copy(
            src_ref=src, dst_ref=dst, send_sem=send, recv_sem=recv,
            device_id={"src": ps, "tgt": pt}, device_id_type=pl.DeviceIdType.MESH,
        )

    def taken(ref, sem):
        pltpu.make_async_copy(ref, ref, sem).wait()

    for ph, pt in peers:
        remote(b_hbm, bb.at[h, t], s_a.at[0], r_a.at[h], ph * g.G + core, pt).start()
    swap = remote(a_hbm, ach.at[core], s_x.at[0], r_x.at[0], sibling, t)
    swap.start()
    pltpu.make_async_copy(b_hbm, bb.at[h, t], r_a.at[h]).start()

    for load in loads[:3]:
        load.wait()
    cpad[...] = jnp.zeros(cpad.shape, F32)
    cpad[:, : cin_ref.shape[1]] = cin_ref[...]
    taps_h, taps_l = split(cpad[...])
    both = jnp.concatenate([taps_h.astype(F32), taps_l.astype(F32)], axis=0).astype(BF16)
    base = dot(both, s1_vm[...])
    H = g.hidden
    row = iota((H, LANES), 0)
    bias = jnp.zeros((H, LANES), F32)
    for n in range(H):
        bias = jnp.where(row == n, bias_ref[n], bias)
    bias_h, bias_l = (part.astype(F32) for part in split(bias))
    bias = jnp.concatenate([bias_h, bias_h, bias_l, bias_l], axis=0)
    bias = jnp.concatenate([bias] * (g.KW // LANES), axis=1)
    bias = jnp.where(iota(bias.shape, 1) == 4 * g.KX + g.rows - 1, bias, 0.0)
    for k in range(g.hk):
        at_k = t * g.kb + (k - 1)
        for l in range(g.hl):
            at_l = s * g.lb + (l - 1)
            parts = []
            for first in (0, H):
                for net in range(2):
                    at = ((k % g.kb * g.lb + l % g.lb) * 2 + net) * g.KW
                    parts.append(base[first : first + H, at : at + g.KW])
            block = jnp.concatenate(parts, axis=0)
            shift = (l // g.lb * g.bk + k // g.kb) * g.block
            if shift:
                block = pltpu.roll(block, shift, 1)
            inside = (at_k >= 0) & (at_k < T * g.kb) & (at_l >= 0) & (at_l < S * g.lb)
            block = (block + bias) * jnp.where(inside, 1.0, 0.0).astype(F32)
            at = (k * g.hl + l) * 2 * H
            w1[at : at + 2 * H, :] = block[: 2 * H, : g.KP].astype(BF16)
            w1[g.M + at : g.M + at + 2 * H, :] = block[2 * H :, : g.KP].astype(BF16)

    loads[3].wait()
    loads[4].wait()
    cpad[:, : cout_ref.shape[1]] = cout_ref[...]
    taps_h, taps_l = split(cpad[...])
    both = jnp.concatenate([taps_h.astype(F32), taps_l.astype(F32)], axis=0).astype(BF16)
    base = dot(both, s2_vm[...])
    blocks = g.hk * g.hl * 2
    for first, at in ((0, 0), (H, g.Y)):
        tall = jnp.concatenate(
            [base[first : first + H, n * LANES : (n + 1) * LANES] for n in range(blocks)], axis=0
        )
        w2[at : at + g.Y, :] = tall.T[: g.Y].astype(BF16)

    tail = g.rows - g.used
    u[:, :, g.used :, :] = jnp.where(
        iota((H2, T, tail, LANES), 2) == tail - 1, jnp.ones((H2, T, tail, LANES), F32), 0.0
    )
    pat[: 3 * g.KX, LANES : 2 * LANES] = jnp.zeros((3 * g.KX, LANES), BF16)
    pat[6 * g.KX :, g.HA * LANES : (g.HA + 1) * LANES] = jnp.zeros((3 * g.KX, LANES), BF16)
    y[:, :LANES] = jnp.zeros((g.Y, LANES), F32)
    y[:, (g.HA + 1) * LANES :] = jnp.zeros((g.Y, LANES), F32)

    loads[5].wait()
    swap.wait_recv()
    if g.pair == LANES:
        a = ach[...].reshape(g.pair, g.C)
    else:
        a = ach[...].astype(F32).reshape(g.pair, g.C)
        a = jnp.concatenate([a] * (LANES // g.pair), axis=0).astype(BF16)

    reach = [slice(1 if pt == 0 else 0, g.bk - 1 if pt == T - 1 else g.bk) for pt in range(T)]
    rows_t = sorted(range(T), key=lambda pt: min(pt, T - 1 - pt))
    at_edge = (t == 0) | (t == T - 1)

    @pl.when(t == 0)
    def _():
        r1[:, :, :, 0] = jnp.zeros((H2, T, 1, g.block, LANES), BF16)
        r2[:, :, :, 0] = jnp.zeros((H2, T, 2, g.block, LANES), BF16)

    @pl.when(t == T - 1)
    def _():
        r1[:, :, :, g.bk - 1] = jnp.zeros((H2, T, 1, g.block, LANES), BF16)
        r2[:, :, :, g.bk - 1] = jnp.zeros((H2, T, 2, g.block, LANES), BF16)

    def source(first, count, pt):
        return vp.at[pl.ds(first, count), pt + reach[pt].start : pt + reach[pt].stop]

    def near(ph, pt):
        return remote(
            source(ph + 1, 1, pt), r1.at[h, t, :, reach[pt]], s_b1.at[0], r_b1.at[h],
            ph * g.G + core, pt,
        )

    def send_other(ph):
        for pt in rows_t:
            remote(
                source(ph + 1 - core, 2, pt), r2.at[h, t, :, reach[pt]], s_b2.at[0], r_b2.at[h],
                ph * g.G + 1 - core, pt,
            ).start()

    for n in range(H2):
        ph = lax.rem(h + H2 - n, H2)
        taken(bb.at[ph], r_a.at[ph])
        for tt in range(T):
            for kk in range(g.kb):
                at = tt * g.block + kk * g.lb
                bf[n, at : at + g.lb, :] = bb[ph, tt, kk].astype(F32)
        vs[n] = lax.dot_general(
            bf[n].astype(BF16), a, (((1,), (1,)), ((), ())), preferred_element_type=F32
        ) * (g.C ** -0.5)
        for tt in range(T):
            vp[ph + 1, tt + 1] = vs[n, tt * g.block : (tt + 1) * g.block, :].astype(BF16)
        for pt in rows_t:
            if n:
                near(ph, pt).start()
                continue

            @pl.when(t != pt)
            def _():
                near(ph, pt).start()

            @pl.when(t == pt)
            def _():
                pltpu.make_async_copy(
                    source(h + 1, 1, pt), r1.at[h, t, :, reach[pt]], r_b1.at[h]
                ).start()

        if n:
            send_other(lax.rem(h + H2 - n + core, H2))
    send_other(lax.rem(h + core, H2))
    for ph, pt in peers:
        pltpu.make_async_copy(b_hbm, b_hbm, s_a.at[0]).wait()
    swap.wait_send()

    lane = iota((g.rows, LANES), 1)
    wide = iota((g.KX, LANES), 1)
    rows_h = g.G * g.rows_i

    def spread(ph):
        ins = []
        for tt in range(T):
            for dt in range(g.bk):
                for ds in range(g.bl):
                    at = (ds * g.bk + dt) * g.block
                    got = r1[ph, tt, 0, dt] if ds == 1 else r2[ph, tt, ds // 2, dt]
                    u[ph, tt, at : at + g.block, :] = got.astype(F32)
            ins.append(u[ph, tt])
        for chunk in range(rows_h):
            x = None
            for tt in range(T):
                shift = (tt - chunk) * g.cols_j % LANES
                moved = pltpu.roll(ins[tt], shift, 1) if shift else ins[tt]
                x = moved if tt == 0 else jnp.where(lane >= tt * g.cols_j, moved, x)
            if g.KX > g.rows:
                x = jnp.concatenate([x, jnp.zeros((g.KX - g.rows, LANES), F32)], axis=0)
            for sh in range(3):
                if sh == 0:
                    moved = jnp.where(wide == 0, 0.0, pltpu.roll(x, 1, 1))
                elif sh == 2:
                    moved = jnp.where(wide == LANES - 1, 0.0, pltpu.roll(x, LANES - 1, 1))
                else:
                    moved = x
                moved = moved.astype(BF16)
                for r in range(3):
                    at = pl.multiple_of((ph * rows_h + chunk + 2 - r) * LANES, LANES)
                    first = (r * 3 + sh) * g.KX
                    pat[first : first + g.KX, pl.ds(at, LANES)] = moved

    def filters(rows):
        if not rows:
            return
        at = [pl.multiple_of((row + 1) * LANES, LANES) for row in rows]
        patch = jnp.concatenate([pat[:, pl.ds(place, LANES)] for place in at], axis=1)
        hid = dot(w1[...], patch)
        hid_h, hid_l = split(jnp.maximum(hid[: g.M] + hid[g.M :], 0.0))
        res = dot(w2[...], hid_h)
        res = res[: g.Y] + res[g.Y :] + dot(w2[: g.Y, :], hid_l)
        for n, place in enumerate(at):
            y[:, pl.ds(place, LANES)] = res[:, n * LANES : (n + 1) * LANES]

    def inner(ph):
        filters([ph * rows_h + n for n in range(1, rows_h - 1)])

    def between(ph):
        row = ph * rows_h + rows_h - 1
        filters([row, lax.rem(row + 1, g.HA)])

    last = iota((g.unit, LANES), 1)

    def finish(ph):
        for n in range(rows_h):
            i = ph * rows_h + n
            sums = []
            for sh in range(3):
                part = None
                for r in range(3):
                    first = (r * 3 + sh) * g.unit
                    at = pl.multiple_of((i + r) * LANES, LANES)
                    term = y[first : first + g.unit, pl.ds(at, LANES)]
                    part = term if part is None else part + term
                sums.append(part)
            res = sums[1]
            res = res + jnp.where(last == 0, 0.0, pltpu.roll(sums[0], 1, 1))
            res = res + jnp.where(last == LANES - 1, 0.0, pltpu.roll(sums[2], LANES - 1, 1))
            for k in range(g.kb):
                for l in range(g.lb):
                    m = k * g.lb + l
                    out_ref[k, l, pl.ds(i, 1), :] = res[m : m + 1, :]

    order = [lax.rem(h + n, H2) for n in range(H2)]
    edge = slice(0, g.bk - 1)
    for n, ph in enumerate(order):
        if n >= 1:
            inner(order[n - 1])
        if n >= 2:
            between(order[n - 2])
        if n >= 3:
            finish(order[n - 2])

        @pl.when(at_edge)
        def _():
            taken(r1.at[ph, :, :, edge], r_b1.at[ph])
            taken(r2.at[ph, :, :, edge], r_b2.at[ph])

        @pl.when(jnp.logical_not(at_edge))
        def _():
            taken(r1.at[ph], r_b1.at[ph])
            taken(r2.at[ph], r_b2.at[ph])

        spread(ph)
    inner(order[-1])
    if H2 > 1:
        between(order[-2])
    between(order[-1])
    for n in range(H2):
        if n == 0 or n >= max(H2 - 2, 1):
            finish(order[n])

    taken(r2.at[:, 1 : T - 1], s_b2.at[0])
    taken(r2.at[:, :2, :, edge], s_b2.at[0])
    for n in range(H2):
        for pt in range(T):
            part = r1.at[0, 0, :, reach[pt]]
            if n:
                taken(part, s_b1.at[0])
                continue

            @pl.when(t != pt)
            def _():
                taken(part, s_b1.at[0])


def per_device(feature_a, feature_b, conv_in, bias_in, conv_out):
    S, T = lax.axis_size("src"), lax.axis_size("tgt")
    g = Plan(S, T, feature_a.shape, feature_b.shape, conv_in.shape[0])
    s1 = jnp.asarray(g.select_in(), BF16)
    s2 = jnp.asarray(g.select_out(), BF16)
    vm = pl.BlockSpec(memory_space=pltpu.VMEM)
    hbm = pl.BlockSpec(memory_space=pl.ANY)
    dma = pltpu.SemaphoreType.DMA
    return pl.pallas_call(
        functools.partial(kernel, g),
        out_shape=jax.ShapeDtypeStruct((g.kb, g.lb, g.HA, g.WA), F32),
        in_specs=[hbm] * 7,
        out_specs=vm,
        scratch_shapes=[
            pltpu.VMEM((g.G,) + feature_a.shape, BF16),
            pltpu.VMEM(conv_in.shape, F32),
            pltpu.SMEM(bias_in.shape, F32),
            pltpu.VMEM(conv_out.shape, F32),
            pltpu.VMEM(s1.shape, BF16),
            pltpu.VMEM(s2.shape, BF16),
            dma((6,)),
            pltpu.VMEM((g.H2, T, g.kb, g.lb, g.C), BF16),
            pltpu.VMEM((g.H2, T * g.block, g.C), F32),
            pltpu.VMEM((g.H2, T * g.block, LANES), F32),
            pltpu.VMEM((g.H2 + 2, T + 2, g.block, LANES), BF16),
            pltpu.VMEM((g.H2, T, 1, g.bk, g.block, LANES), BF16),
            pltpu.VMEM((g.H2, T, 2, g.bk, g.block, LANES), BF16),
            pltpu.VMEM((g.H2, T, g.rows, LANES), F32),
            pltpu.VMEM((g.KP, (g.HA + 2) * LANES), BF16),
            pltpu.VMEM((2 * g.M, g.KP), BF16),
            pltpu.VMEM((2 * g.Y, g.M), BF16),
            pltpu.VMEM((g.Y, (g.HA + 2) * LANES), F32),
            pltpu.VMEM((g.hidden, LANES), F32),
            dma((1,)),
            dma((1,)),
            dma((1,)),
            dma((g.H2,)),
            dma((1,)),
            dma((1,)),
            dma((g.H2,)),
            dma((g.H2,)),
        ],
        compiler_params=pltpu.CompilerParams(
            collective_id=0, has_side_effects=True, vmem_limit_bytes=62 * 1024 * 1024
        ),
    )(feature_a, feature_b, conv_in, bias_in, conv_out, s1, s2)


def solution(mesh):
    in_specs = (P("src", "tgt", None), P("tgt", "src", None), P(), P(), P())
    out_specs = P("tgt", "src", None, None)
    return jax.shard_map(
        per_device, mesh=mesh, in_specs=in_specs, out_specs=out_specs, check_vma=False
    )
```
